256 devices in a mesh: pipe: 16 (over x, y_lo, core), tensor: 16 (over z, y_hi).
Axes of the slice: x: 4, y: 4 (y_hi: 2, y_lo: 2; y = y_hi * 2 + y_lo), z: 8, core: 2. Of those that a mesh axis runs over, the one named last changes fastest.
Arguments:
- q_fwd: bfloat16 [16, 256, 6144], P('pipe', None, 'tensor'), may hold values from -9 to 9
- k_fwd: bfloat16 [16, 256, 6144], P('pipe', None, 'tensor'), may hold values from -4 to 4
- v_fwd: bfloat16 [16, 256, 6144], P('pipe', None, 'tensor'), may hold values from -6 to 6
- q_park: bfloat16 [16, 256, 6144], P('pipe', None, 'tensor'), may hold values from -9 to 9
- k_park: bfloat16 [16, 256, 6144], P('pipe', None, 'tensor'), may hold values from -4 to 4
- v_park: bfloat16 [16, 256, 6144], P('pipe', None, 'tensor'), may hold values from -6 to 6
- resid: bfloat16 [16, 256, 12288], P('pipe', 'tensor'), may hold values from -6 to 6
- out_weight: bfloat16 [16, 6144, 12288], P('pipe', 'tensor'), may hold values from -0.078125 to 0.078125
- cotangent: bfloat16 [16, 256, 12288], P('pipe', 'tensor'), may hold values from -6 to 6
Outputs:
- output: bfloat16 [16, 256, 12288], P('pipe', 'tensor')
- grad_q: bfloat16 [16, 256, 6144], P('pipe', None, 'tensor')
- grad_k: bfloat16 [16, 256, 6144], P('pipe', None, 'tensor')
- grad_v: bfloat16 [16, 256, 6144], P('pipe', None, 'tensor')
- evict_q: bfloat16 [16, 256, 6144], P('pipe', None, 'tensor')
- evict_k: bfloat16 [16, 256, 6144], P('pipe', None, 'tensor')
- evict_v: bfloat16 [16, 256, 6144], P('pipe', None, 'tensor')
The draws below stay inside these ranges and needn't reach their ends.
All inputs are finite; a program needn't handle non-finite values.
Results may differ from the reference program's by a relative error of at most 0.025.
Values may be sent and summed in bfloat16 or wider, within the bound.
A program may use at most 128 MiB of HBM per device.

```python
import jax
import jax.numpy as jnp
from jax import lax

D = 12288
HEADS = 48
HEAD = 128
S = 256
HD = 6144
N_PIPE = 16
N_TENSOR = 16


def draw_pair(key, aligned_on):
    subkeys = jax.random.split(key, 7)
    extent = (N_PIPE, S, HD)
    drawn_q = jnp.clip(jax.random.normal(subkeys[0], extent, jnp.float32), -4.0, 4.0)
    drawn_k = jnp.clip(jax.random.normal(subkeys[1], extent, jnp.float32), -4.0, 4.0)
    flat_q = drawn_q
    flat_k = drawn_k
    row_index = jnp.arange(S)
    aligned = jnp.logical_and((row_index % 32 == 31)[None, :, None], aligned_on > 0.5)
    preceding = jnp.logical_and((row_index % 32 == 30)[None, :, None], aligned_on > 0.5)
    strong = jax.random.uniform(subkeys[4], extent, jnp.float32, 2.5, 3.5) * jnp.sign(jax.random.normal(subkeys[5], extent, jnp.float32))
    strength = jax.random.uniform(subkeys[6], (N_PIPE, S, 1), jnp.float32, 1.0, 2.5)
    following = jnp.roll(strong, -1, axis=1)
    keys_out = jnp.where(aligned, strong, flat_k)
    keys_out = jnp.where(preceding, 0.99 * following, keys_out)
    queries_out = jnp.where(aligned, strong * strength, flat_q)
    return (queries_out, keys_out)


def draw_q_fwd(key, part):
    own_key = jax.random.fold_in(key, 11)
    return draw_pair(own_key, 0.0)[0].astype(jnp.bfloat16)


def draw_k_fwd(key, part):
    own_key = jax.random.fold_in(key, 11)
    return draw_pair(own_key, 0.0)[1].astype(jnp.bfloat16)


def draw_q_park(key, part):
    own_key = jax.random.fold_in(key, 12)
    return draw_pair(own_key, 0.0)[0].astype(jnp.bfloat16)


def draw_k_park(key, part):
    own_key = jax.random.fold_in(key, 12)
    return draw_pair(own_key, 0.0)[1].astype(jnp.bfloat16)


def shard_levels(key, dims, shards, low, top_value):
    gain, own = 1.0, jax.random.fold_in(key, 6)
    for axis_at, parts in shards:
        draws = jnp.exp(jax.random.uniform(jax.random.fold_in(own, axis_at), (parts,), jnp.float32, low / len(shards), top_value / len(shards)))
        gain = gain * jnp.repeat(draws, dims[axis_at] // parts).reshape([-1 if axis == axis_at else 1 for axis in range(len(dims))])
    return gain


def bell_draw(rng, shape, width, reach, cuts=(), held_as=jnp.bfloat16):
    loudness = shard_levels(rng, shape, cuts, -0.22, 0.18) if cuts else 1.0
    entries = jax.random.normal(rng, shape, jnp.float32) * width * loudness
    return jnp.minimum(jnp.maximum(entries, -reach), reach).astype(held_as)


def setup_inputs(seed: int = 0) -> dict:
    seeds = jax.random.split(jax.random.key(seed), 10)
    q_fwd = draw_q_fwd(jax.random.fold_in(seeds[9], 71), 0)
    k_fwd = draw_k_fwd(jax.random.fold_in(seeds[9], 71), 0)
    v_fwd = bell_draw(seeds[2], (N_PIPE, S, HD), 1.0, 6.0, ((0, 16), (2, 16)))
    q_park = draw_q_park(jax.random.fold_in(seeds[9], 71), 0)
    k_park = draw_k_park(jax.random.fold_in(seeds[9], 71), 0)
    v_park = bell_draw(seeds[5], (N_PIPE, S, HD), 1.0, 6.0, ((0, 16), (2, 16)))
    resid = bell_draw(seeds[6], (N_PIPE, S, D), 1.0, 6.0, ((0, 16), (1, 16)))
    out_weight = bell_draw(seeds[7], (N_PIPE, HD, D), HD ** -0.5, 0.078125, ((0, 16), (1, 16)))
    cotangent = bell_draw(seeds[8], (N_PIPE, S, D), 1.0, 6.0, ((0, 16), (1, 16)))
    return dict(q_fwd=q_fwd, k_fwd=k_fwd, v_fwd=v_fwd, q_park=q_park, k_park=k_park, v_park=v_park, resid=resid, out_weight=out_weight, cotangent=cotangent)


def probabilities(queries, keys_in):
    seq_length = queries.shape[0]
    head_width = queries.shape[-1]
    scores = jnp.einsum("qhd,khd->hqk", queries.astype(jnp.float32), keys_in.astype(jnp.float32)) * (head_width ** -0.5)
    causal = lax.broadcasted_iota(jnp.int32, (seq_length, seq_length), 0) >= lax.broadcasted_iota(jnp.int32, (seq_length, seq_length), 1)
    scores = jnp.where(causal[None], scores, jnp.float32(-1e30))
    biggest = jnp.max(scores, axis=-1, keepdims=True)
    exponent = jnp.exp(scores - biggest)
    attn_probs = exponent / jnp.sum(exponent, axis=-1, keepdims=True)
    return attn_probs, attn_probs.astype(jnp.bfloat16)


def split_heads(block):
    return block.reshape(block.shape[0], HEADS, HEAD)


def section_forward(queries, keys_in, values, residual, weight):
    attn_probs, attn_low = probabilities(split_heads(queries), split_heads(keys_in))
    context = jnp.einsum("hqk,khd->qhd", attn_low.astype(jnp.float32), split_heads(values).astype(jnp.float32))
    context = context.astype(jnp.bfloat16).reshape(S, HD)
    group_width = HD // N_TENSOR
    full_sum = jnp.zeros((S, D), jnp.float32)
    for group in range(N_TENSOR):
        part_low = jnp.dot(context[:, group * group_width:(group + 1) * group_width], weight[group * group_width:(group + 1) * group_width], preferred_element_type=jnp.float32).astype(jnp.bfloat16)
        full_sum = full_sum + lax.optimization_barrier(part_low).astype(jnp.float32)
    return (residual.astype(jnp.float32) + full_sum).astype(jnp.bfloat16)


def section_backward(queries, keys_in, values, grad_out, weight):
    grad_ctx = lax.dot_general(grad_out, weight, (((1,), (1,)), ((), ())), preferred_element_type=jnp.float32).astype(jnp.bfloat16)
    q_heads, k_heads, v_heads = split_heads(queries), split_heads(keys_in), split_heads(values)
    grad_heads = split_heads(grad_ctx)
    attn_probs, attn_low = probabilities(q_heads, k_heads)
    recon = jnp.einsum("hqk,khd->qhd", attn_low.astype(jnp.float32), v_heads.astype(jnp.float32)).astype(jnp.bfloat16)
    row_dots = jnp.sum(grad_heads.astype(jnp.float32) * recon.astype(jnp.float32), axis=-1)
    row_dots = jnp.transpose(row_dots)[:, :, None]
    grad_probs = jnp.einsum("qhd,khd->hqk", grad_heads.astype(jnp.float32), v_heads.astype(jnp.float32))
    grad_scores = (attn_probs * (grad_probs - row_dots)).astype(jnp.bfloat16).astype(jnp.float32)
    scale = HEAD ** -0.5
    grad_query = (jnp.einsum("hqk,khd->qhd", grad_scores, k_heads.astype(jnp.float32)) * scale).astype(jnp.bfloat16)
    grad_key = (jnp.einsum("hqk,qhd->khd", grad_scores, q_heads.astype(jnp.float32)) * scale).astype(jnp.bfloat16)
    grad_value = jnp.einsum("hqk,qhd->khd", attn_low.astype(jnp.float32), grad_heads.astype(jnp.float32)).astype(jnp.bfloat16)
    return grad_query.reshape(S, HD), grad_key.reshape(S, HD), grad_value.reshape(S, HD)


def reference(q_fwd, k_fwd, v_fwd, q_park, k_park, v_park, resid, out_weight, cotangent):
    outputs, grads_q, grads_k, grads_v = [], [], [], []
    for section in range(N_PIPE):
        mirror_row = N_PIPE - 1 - section
        outputs.append(section_forward(q_fwd[section], k_fwd[section], v_fwd[section], resid[section], out_weight[section]))
        grad_query, grad_key, grad_value = section_backward(q_park[mirror_row], k_park[mirror_row], v_park[mirror_row], cotangent[section], out_weight[section])
        grads_q.append(grad_query)
        grads_k.append(grad_key)
        grads_v.append(grad_value)
    return (jnp.stack(outputs), jnp.stack(grads_q), jnp.stack(grads_k), jnp.stack(grads_v), q_fwd[::-1], k_fwd[::-1], v_fwd[::-1])
```

```python
import jax
import jax.numpy as jnp
from jax import lax
from jax.experimental import pallas as pl
from jax.experimental.pallas import tpu as pltpu
from jax.sharding import PartitionSpec as P

HEAD = 128
MESH = pl.DeviceIdType.MESH
CUT = 5120
TILE = 512
ORDER = (7, 1, 6, 2, 5, 3, 0, 4)


def slot(off, side):
    return 2 * ORDER.index(off % 8) + side


def kernel(
    q_in, k_in, v_in, qp_in, kp_in, vp_in, resid_in, w_in, cot_in,
    out_ref, gq_ref, gk_ref, gv_ref, eq_ref, ek_ref, ev_ref,
    w, g, part, za, zb, ya, yb, qf, kf, vf, qs, ks, vs, resid, ctx, ctxp, probs, recon, gctx, gout, out,
    load_sem, store_sem, agz_s, agz_r, agy_s, agy_r, rsz_s, rsz_r, rsy_s, rsy_r, mir_s, mir_r,
):
    width = w.shape[1]
    rows = resid.shape[0]
    seq = qf.shape[0]
    heads = qf.shape[1] // HEAD
    wide_b = width - CUT
    p, t = lax.axis_index("pipe"), lax.axis_index("tensor")
    z, line = lax.div(t, 2), lax.rem(t, 2)
    up = (p, lax.rem(z + 1, 8) * 2 + line)
    down = (p, lax.rem(z + 7, 8) * 2 + line)
    across = (p, z * 2 + 1 - line)
    mirror = (lax.axis_size("pipe") - 1 - p, t)
    ways = (up, down)

    def row_of(off, side):
        block = lax.rem(z + off % 8, 8) * 2 + lax.rem(line + side, 2)
        return pl.multiple_of(block * rows, rows)

    loads = {}

    def load(name, src, dst):
        loads[name] = pltpu.make_async_copy(src, dst, load_sem.at[len(loads)])
        loads[name].start()

    load("cot", cot_in.at[0], g.at[slot(0, 0)])
    load("q", q_in.at[0], qf)
    load("k", k_in.at[0], kf)
    load("v", v_in.at[0], vf)
    quarter = w.shape[0] // 4
    for i in range(4):
        load(f"w{i}", w_in.at[0, pl.ds(i * quarter, quarter)], w.at[pl.ds(i * quarter, quarter)])
    load("resid", resid_in.at[0], resid)

    def remote(src, dst, send, recv, device):
        return pltpu.make_async_remote_copy(
            src_ref=src, dst_ref=dst, send_sem=send, recv_sem=recv, device_id=device, device_id_type=MESH
        )

    cols_a = pl.ds(0, CUT)
    cols_b = pl.ds(CUT, wide_b)
    half_a = (pl.ds(0, CUT // 2), pl.ds(CUT // 2, CUT // 2))
    half_b = (pl.ds(CUT, wide_b // 2), pl.ds(CUT + wide_b // 2, wide_b // 2))
    half_zb = (pl.ds(0, wide_b // 2), pl.ds(wide_b // 2, wide_b // 2))
    sides = (0, 0, 1)

    agz, rsz = {}, {}
    for way in range(2):
        sign = -1 if way == 0 else 1
        for hop in range(4):
            for stream in range(3):
                n = (way * 4 + hop) * 3 + stream
                side = sides[stream]
                if hop < 3:
                    cols = cols_a if stream == 0 else cols_b
                else:
                    cols = half_a[way] if stream == 0 else half_b[way]
                agz[way, hop, stream] = remote(
                    g.at[slot(sign * hop, side), :, cols],
                    g.at[slot(sign * (hop + 1), side), :, cols],
                    agz_s.at[n], agz_r.at[n], ways[way],
                )
                if hop > 0:
                    cols = cols_a if stream == 0 else cols_b
                    land = za.at[way, hop] if stream == 0 else zb.at[way, hop, side]
                else:
                    cols = half_a[way] if stream == 0 else half_b[way]
                    land = za.at[way, hop, :, half_a[way]] if stream == 0 else zb.at[way, hop, side, :, half_zb[way]]
                rsz[way, hop, stream] = remote(
                    part.at[slot(-sign * (4 - hop), side), :, cols], land, rsz_s.at[n], rsz_r.at[n], ways[way]
                )
    agy, rsy = {}, {}
    for i, off in enumerate((0, 7, 1, 6, 2, 5, 3)):
        agy[off] = remote(
            g.at[slot(off, 0), :, cols_a], g.at[slot(off, 1), :, cols_a], agy_s.at[i], agy_r.at[i], across
        )
    for way in range(2):
        agy[4, way] = remote(
            g.at[slot(4, 0), :, half_a[way]], g.at[slot(4, 1), :, half_a[way]],
            agy_s.at[7 + way], agy_r.at[7 + way], across,
        )
    agy["b"] = remote(g.at[slot(0, 0), :, cols_b], g.at[slot(0, 1), :, cols_b], agy_s.at[9], agy_r.at[9], across)
    for off in range(8):
        rsy[off] = remote(part.at[slot(off, 1), :, cols_a], ya.at[off], rsy_s.at[off], rsy_r.at[off], across)
    rsy["b"] = remote(part.at[slot(0, 1), :, cols_b], yb, rsy_s.at[8], rsy_r.at[8], across)
    mir = [
        remote(src, dst, mir_s.at[i], mir_r.at[i], mirror)
        for i, (src, dst) in enumerate((
            (qp_in.at[0], qs), (kp_in.at[0], ks), (vp_in.at[0], vs),
            (q_in.at[0], eq_ref.at[0]), (k_in.at[0], ek_ref.at[0]), (v_in.at[0], ev_ref.at[0]),
        ))
    ]

    scale = HEAD**-0.5

    def softmax(queries, keys):
        scores = lax.dot_general(queries, keys, (((1,), (1,)), ((), ())), preferred_element_type=jnp.float32) * scale
        seen = lax.broadcasted_iota(jnp.int32, (seq, seq), 0) >= lax.broadcasted_iota(jnp.int32, (seq, seq), 1)
        scores = jnp.where(seen, scores, jnp.float32(-1e30))
        grown = jnp.exp(scores - jnp.max(scores, axis=-1, keepdims=True))
        return grown / jnp.sum(grown, axis=-1, keepdims=True)

    def forward_attention():
        for h in range(heads):
            cols = pl.ds(h * HEAD, HEAD)
            low = softmax(qf[:, cols], kf[:, cols]).astype(jnp.bfloat16)
            ctx[:, cols] = jnp.dot(low, vf[:, cols], preferred_element_type=jnp.float32).astype(jnp.bfloat16)
        for off in range(8):
            for side in range(2):
                ctxp[pl.ds(slot(off, side) * rows, rows), :] = ctx[pl.ds(row_of(off, side), rows), :]

    def project(first, last):
        @pl.loop(first // TILE, last // TILE)
        def _(i):
            cols = pl.ds(pl.multiple_of(i * TILE, TILE), TILE)
            made = jnp.dot(ctxp[...], w[:, cols], preferred_element_type=jnp.float32).astype(jnp.bfloat16)
            part[:, :, cols] = made.reshape(part.shape[0], rows, TILE)

    def gather_grad(group):
        def body(i, total):
            cols = pl.ds(pl.multiple_of(i * 1024, 1024), 1024)
            block = g[pl.ds(group * 4, 4), :, cols].reshape(4 * rows, 1024)
            return total + lax.dot_general(
                block, w[:, cols], (((1,), (1,)), ((), ())), preferred_element_type=jnp.float32
            )

        total = lax.fori_loop(0, width // 1024, body, jnp.zeros((4 * rows, w.shape[0]), jnp.float32))
        total = total.astype(jnp.bfloat16)
        for i in range(4):
            off, side = ORDER[2 * group + i // 2], i % 2
            gctx[pl.ds(row_of(off, side), rows), :] = total[i * rows : (i + 1) * rows]

    def stash_probs():
        for h in range(heads):
            cols = pl.ds(h * HEAD, HEAD)
            attn = softmax(qs[:, cols], ks[:, cols])
            probs[h] = attn
            recon[:, cols] = jnp.dot(
                attn.astype(jnp.bfloat16), vs[:, cols], preferred_element_type=jnp.float32
            ).astype(jnp.bfloat16)

    def backward_attention():
        for h in range(heads):
            cols = pl.ds(h * HEAD, HEAD)
            grad, attn = gctx[:, cols], probs[h]
            dots = jnp.sum(
                grad.astype(jnp.float32) * recon[:, cols].astype(jnp.float32), axis=-1, keepdims=True
            )
            grad_probs = lax.dot_general(
                grad, vs[:, cols], (((1,), (1,)), ((), ())), preferred_element_type=jnp.float32
            )
            grad_scores = (attn * (grad_probs - dots)).astype(jnp.bfloat16)
            gout[0, :, cols] = (
                jnp.dot(grad_scores, ks[:, cols], preferred_element_type=jnp.float32) * scale
            ).astype(jnp.bfloat16)
            gout[1, :, cols] = (
                lax.dot_general(
                    grad_scores, qs[:, cols], (((0,), (0,)), ((), ())), preferred_element_type=jnp.float32
                )
                * scale
            ).astype(jnp.bfloat16)
            gout[2, :, cols] = lax.dot_general(
                attn.astype(jnp.bfloat16), grad, (((0,), (0,)), ((), ())), preferred_element_type=jnp.float32
            ).astype(jnp.bfloat16)

    def add(dst, terms, first, last):
        @pl.loop(0, (last - first) // TILE)
        def _(i):
            at = first + i * TILE
            total = part[dst, :, pl.ds(pl.multiple_of(at, TILE), TILE)].astype(jnp.float32)
            for ref, shift in terms:
                total += ref[:, pl.ds(pl.multiple_of(at - shift, TILE), TILE)].astype(jnp.float32)
            part[dst, :, pl.ds(pl.multiple_of(at, TILE), TILE)] = total.astype(jnp.bfloat16)

    def reduce_a(hop):
        if hop == 0:
            rsy[4].wait_recv()
            add(slot(4, 0), [(ya.at[4], 0)], 0, CUT)
        for way in range(2):
            sign = -1 if way == 0 else 1
            off = (-sign * (4 - hop)) % 8
            if hop > 0:
                rsy[off].wait_recv()
                rsz[way, hop - 1, 0].wait_recv()
                if hop == 1:
                    middle = CUT // 2
                    first, last = (0, middle) if way == 0 else (middle, CUT)
                    add(slot(off, 0), [(ya.at[off], 0), (za.at[way, 0], 0)], first, last)
                    first, last = (middle, CUT) if way == 0 else (0, middle)
                    add(slot(off, 0), [(ya.at[off], 0)], first, last)
                else:
                    add(slot(off, 0), [(ya.at[off], 0), (za.at[way, hop - 1], 0)], 0, CUT)
            rsz[way, hop, 0].start()

    def reduce_b(hop, stream):
        side = sides[stream]
        for way in range(2):
            sign = -1 if way == 0 else 1
            off = (-sign * (4 - hop)) % 8
            if hop > 0:
                rsz[way, hop - 1, stream].wait_recv()
                middle = CUT + wide_b // 2
                first, last = CUT, width
                if hop == 1:
                    first, last = (CUT, middle) if way == 0 else (middle, width)
                add(slot(off, side), [(zb.at[way, hop - 1, side], CUT)], first, last)
            rsz[way, hop, stream].start()

    def gather_on(hop, stream):
        for way in range(2):
            sign = -1 if way == 0 else 1
            agz[way, hop, stream].wait_recv()
            if hop < 3:
                agz[way, hop + 1, stream].start()
            if stream == 0:
                agy[sign * (hop + 1) % 8 if hop < 3 else (4, way)].start()

    barrier = pltpu.get_barrier_semaphore()
    for device in (up, down, across, mirror):
        pl.semaphore_signal(barrier, inc=1, device_id=device, device_id_type=MESH)
    pl.semaphore_wait(barrier, 4)

    loads["cot"].wait()
    for way in range(2):
        for stream in range(2):
            agz[way, 0, stream].start()
    agy["b"].start()
    agy[0].start()
    for i in range(3):
        mir[i].start()

    for name in ("q", "k", "v"):
        loads[name].wait()
    forward_attention()
    agy["b"].wait_recv()
    for way in range(2):
        agz[way, 0, 2].start()
    for i in range(4):
        loads[f"w{i}"].wait()
    project(0, CUT)
    for off in (4, 3, 5, 2, 6, 1, 7, 0):
        rsy[off].start()
    project(CUT, width)
    reduce_b(0, 1)
    reduce_b(0, 2)

    for hop in range(4):
        for stream in range(3):
            gather_on(hop, stream)
        reduce_a(hop)
        if hop < 3:
            reduce_b(hop + 1, 1)
            reduce_b(hop + 1, 2)
        if hop == 0:
            for i in range(3, 6):
                mir[i].start()
        if hop == 1:
            agy[7].wait_recv()
            agy[1].wait_recv()
            gather_grad(0)
        if hop == 2:
            for i in range(3):
                mir[i].wait_recv()
            stash_probs()
            agy[6].wait_recv()
            agy[2].wait_recv()
            gather_grad(1)

    for way in range(2):
        rsz[way, 3, 2].wait_recv()
    add(slot(0, 1), [(zb.at[0, 3, 1], CUT), (zb.at[1, 3, 1], CUT)], CUT, width)
    rsy["b"].start()
    agy[5].wait_recv()
    agy[3].wait_recv()
    gather_grad(2)
    agy[0].wait_recv()
    for way in range(2):
        agy[4, way].wait_recv()
    gather_grad(3)
    backward_attention()
    stores = [
        pltpu.make_async_copy(gout.at[i], ref.at[0], store_sem.at[i]) for i, ref in enumerate((gq_ref, gk_ref, gv_ref))
    ]
    for copy in stores:
        copy.start()

    loads["resid"].wait()
    rsy[0].wait_recv()
    for way in range(2):
        rsz[way, 3, 0].wait_recv()
        rsz[way, 3, 1].wait_recv()
    rsy["b"].wait_recv()

    def finish(first, last, refs, shift):
        @pl.loop(0, (last - first) // TILE)
        def _(i):
            cols = pl.ds(pl.multiple_of(first + i * TILE, TILE), TILE)
            total = part[slot(0, 0), :, cols].astype(jnp.float32)
            for ref in refs:
                total += ref[:, pl.ds(pl.multiple_of(first - shift + i * TILE, TILE), TILE)].astype(jnp.float32)
            out[:, cols] = (resid[:, cols].astype(jnp.float32) + total).astype(jnp.bfloat16)

    finish(0, CUT, (ya.at[0], za.at[0, 3], za.at[1, 3]), 0)
    finish(CUT, width, (yb, zb.at[0, 3, 0], zb.at[1, 3, 0]), CUT)
    last = pltpu.make_async_copy(out, out_ref.at[0], store_sem.at[3])
    last.start()

    for i in range(3, 6):
        mir[i].wait_recv()
    for copies in (agz, rsz, agy, rsy):
        for copy in copies.values():
            copy.wait_send()
    for copy in mir:
        copy.wait_send()
    for copy in stores:
        copy.wait()
    last.wait()


def per_device(q_fwd, k_fwd, v_fwd, q_park, k_park, v_park, resid, out_weight, cotangent):
    seq, features = q_fwd.shape[1:]
    rows, width = resid.shape[1:]
    slots = seq // rows
    heads = features // HEAD
    low = jnp.bfloat16
    block = jax.ShapeDtypeStruct(q_fwd.shape, low)
    anywhere = pl.BlockSpec(memory_space=pl.ANY)
    sems = pltpu.SemaphoreType.DMA
    return pl.pallas_call(
        kernel,
        name="relay",
        out_shape=(jax.ShapeDtypeStruct(resid.shape, low),) + (block,) * 6,
        in_specs=[anywhere] * 9,
        out_specs=(anywhere,) * 7,
        scratch_shapes=[
            pltpu.VMEM((features, width), low),
            pltpu.VMEM((slots, rows, width), low),
            pltpu.VMEM((slots, rows, width), low),
            pltpu.VMEM((2, 4, rows, CUT), low),
            pltpu.VMEM((2, 4, 2, rows, width - CUT), low),
            pltpu.VMEM((8, rows, CUT), low),
            pltpu.VMEM((rows, width - CUT), low),
            *[pltpu.VMEM((seq, features), low) for _ in range(6)],
            pltpu.VMEM((rows, width), low),
            pltpu.VMEM((seq, features), low),
            pltpu.VMEM((seq, features), low),
            pltpu.VMEM((heads, seq, seq), jnp.float32),
            pltpu.VMEM((seq, features), low),
            pltpu.VMEM((seq, features), low),
            pltpu.VMEM((3, seq, features), low),
            pltpu.VMEM((rows, width), low),
            sems((9,)), sems((4,)), sems((24,)), sems((24,)), sems((10,)), sems((10,)),
            sems((24,)), sems((24,)), sems((9,)), sems((9,)), sems((6,)), sems((6,)),
        ],
        compiler_params=pltpu.CompilerParams(
            collective_id=0, has_side_effects=True, vmem_limit_bytes=56 * 2**20
        ),
    )(q_fwd, k_fwd, v_fwd, q_park, k_park, v_park, resid, out_weight, cotangent)


def solution(mesh):
    placed = (P("pipe", None, "tensor"),) * 6 + (P("pipe", "tensor", None),) * 3
    return jax.shard_map(
        per_device,
        mesh=mesh,
        in_specs=placed,
        out_specs=(P("pipe", "tensor", None),) + (P("pipe", None, "tensor"),) * 6,
        check_vma=False,
    )
```

```python
import jax
import jax.numpy as jnp
from jax import lax
from jax.experimental import pallas as pl
from jax.experimental.pallas import tpu as pltpu
from jax.sharding import PartitionSpec as P

HEAD = 128
MESH = pl.DeviceIdType.MESH
CUT = 5120
TILE = 1024
STEP = 512
PLAN = (
    ("cross",), ("cross0",), ("send", 0, 1), ("send", 1, 1), ("forward",), ("send", 1, 0), ("send", 0, 0),
    ("mirror", 2), ("gather", 0, 1, 0), ("gather", 0, 1, 1), ("project_b",), ("project_a",), ("reduce_b", 0, 1, 0),
    ("mirror", 3), ("part", 4), ("crossed",), ("part", 2), ("part", 3), ("gather", 1, 1, 1), ("gather", 0, 0, 1),
    ("reduce_b", 0, 2, 0), ("reduce_b", 1, 1, 0), ("mirror", 0), ("gather", 0, 0, 0), ("gather", 0, 2, 1),
    ("gather", 2, 1, 1), ("gather", 1, 1, 0), ("reduce_b", 0, 2, 1), ("gather", 1, 0, 1), ("reduce_a0",),
    ("reduce_b", 0, 1, 1), ("gather", 1, 0, 0), ("reduce_b", 1, 2, 1), ("gather", 0, 2, 0), ("reduce_a", 1, 0),
    ("mirror", 5), ("part", 5), ("mirror", 1), ("gather", 1, 2, 1), ("gather", 2, 1, 0), ("part", 0), ("part", 6),
    ("reduce_b", 1, 1, 1), ("gather", 2, 0, 1), ("reduce_b", 1, 2, 0), ("gather", 1, 2, 0), ("reduce_b", 2, 2, 1),
    ("reduce_a", 1, 1), ("reduce_b", 2, 2, 0), ("reduce_b", 2, 1, 1), ("gather", 3, 1, 1), ("gather", 3, 0, 1),
    ("gather", 2, 0, 0), ("gather", 2, 2, 1), ("gather", 2, 2, 0), ("part", 7), ("stash",), ("gather", 3, 1, 0),
    ("reduce_b", 2, 1, 0), ("gather", 3, 0, 0), ("reduce_a", 2, 1), ("reduce_b", 3, 2, 0), ("reduce_b", 3, 2, 1),
    ("mirror", 4), ("reduce_a", 2, 0), ("grad_a",), ("gather", 3, 2, 0), ("reduce_a", 3, 1), ("gather", 3, 2, 1),
    ("part", 1), ("reduce_b", 3, 1, 0), ("sum_b",), ("reduce_b", 3, 1, 1), ("reduce_a", 3, 0), ("grad_b",),
    ("backward",),
)


def slot(off, side):
    return side * 8 + off % 8


def kernel(
    q_in, k_in, v_in, qp_in, kp_in, vp_in, resid_in, w_in, cot_in,
    out_ref, gq_ref, gk_ref, gv_ref, eq_ref, ek_ref, ev_ref,
    w, g, part, za, zb, ya, yb, qf, kf, vf, qs, ks, vs, parked, evicted, resid, ctx, ctxp, probs, recon, total, gctx, gout, out,
    load_sem, store_sem, agz_s, agz_r, agy_s, agy_r, rsz_s, rsz_r, rsy_s, rsy_r, mir_s, mir_r,
):
    width = w.shape[1]
    rows = resid.shape[0]
    seq = qf.shape[0]
    heads = qf.shape[1] // HEAD
    wide_b = width - CUT
    p, t = lax.axis_index("pipe"), lax.axis_index("tensor")
    z, line = lax.div(t, 2), lax.rem(t, 2)
    up = (p, lax.rem(z + 1, 8) * 2 + line)
    down = (p, lax.rem(z + 7, 8) * 2 + line)
    across = (p, z * 2 + 1 - line)
    mirror = (lax.axis_size("pipe") - 1 - p, t)
    ways = (up, down)

    def row_of(off, side):
        block = lax.rem(z + off % 8, 8) * 2 + lax.rem(line + side, 2)
        return pl.multiple_of(block * rows, rows)

    loads = {}

    def load(name, src, dst):
        loads[name] = pltpu.make_async_copy(src, dst, load_sem.at[len(loads)])
        loads[name].start()

    load("cot", cot_in.at[0], g.at[slot(0, 0)])
    for i, ref in enumerate((qp_in, kp_in, vp_in)):
        load(f"p{i}", ref.at[0], parked.at[i])
    load("q", q_in.at[0], qf)
    load("k", k_in.at[0], kf)
    load("v", v_in.at[0], vf)
    quarter = w.shape[0] // 4
    for i in range(4):
        load(f"w{i}", w_in.at[0, pl.ds(i * quarter, quarter)], w.at[pl.ds(i * quarter, quarter)])
    load("resid", resid_in.at[0], resid)

    def remote(src, dst, send, recv, device):
        return pltpu.make_async_remote_copy(
            src_ref=src, dst_ref=dst, send_sem=send, recv_sem=recv, device_id=device, device_id_type=MESH
        )

    cols_a = pl.ds(0, CUT)
    cols_b = pl.ds(CUT, wide_b)
    half_a = (pl.ds(0, CUT // 2), pl.ds(CUT // 2, CUT // 2))
    half_b = (pl.ds(CUT, wide_b // 2), pl.ds(CUT + wide_b // 2, wide_b // 2))
    half_zb = (pl.ds(0, wide_b // 2), pl.ds(wide_b // 2, wide_b // 2))
    sides = (0, 0, 1)

    agz, rsz = {}, {}
    for way in range(2):
        sign = -1 if way == 0 else 1
        for hop in range(4):
            for stream in range(3):
                n = (way * 4 + hop) * 3 + stream
                side = sides[stream]
                if hop < 3:
                    cols = cols_a if stream == 0 else cols_b
                else:
                    cols = half_a[way] if stream == 0 else half_b[way]
                agz[way, hop, stream] = remote(
                    g.at[slot(sign * hop, side), :, cols],
                    g.at[slot(sign * (hop + 1), side), :, cols],
                    agz_s.at[n], agz_r.at[n], ways[way],
                )
                if hop > 0:
                    cols = cols_a if stream == 0 else cols_b
                    land = za.at[way, hop] if stream == 0 else zb.at[way, hop, side]
                else:
                    cols = half_a[way] if stream == 0 else half_b[way]
                    land = za.at[way, hop, :, half_a[way]] if stream == 0 else zb.at[way, hop, side, :, half_zb[way]]
                rsz[way, hop, stream] = remote(
                    part.at[slot(-sign * (4 - hop), side), :, cols], land, rsz_s.at[n], rsz_r.at[n], ways[way]
                )
    agy, rsy = {}, {}
    for i, off in enumerate((0, 7, 1, 6, 2, 5, 3)):
        agy[off] = remote(
            g.at[slot(off, 0), :, cols_a], g.at[slot(off, 1), :, cols_a], agy_s.at[i], agy_r.at[i], across
        )
    for way in range(2):
        agy[4, way] = remote(
            g.at[slot(4, 0), :, half_a[way]], g.at[slot(4, 1), :, half_a[way]],
            agy_s.at[7 + way], agy_r.at[7 + way], across,
        )
    agy["b"] = remote(g.at[slot(0, 0), :, cols_b], g.at[slot(0, 1), :, cols_b], agy_s.at[9], agy_r.at[9], across)
    for off in range(8):
        rsy[off] = remote(part.at[slot(off, 1), :, cols_a], ya.at[off], rsy_s.at[off], rsy_r.at[off], across)
    rsy["b"] = remote(part.at[slot(0, 1), :, cols_b], yb, rsy_s.at[8], rsy_r.at[8], across)
    mir = [
        remote(src, dst, mir_s.at[i], mir_r.at[i], mirror)
        for i, (src, dst) in enumerate((
            (parked.at[0], qs), (parked.at[1], ks), (parked.at[2], vs),
            (qf, evicted.at[0]), (kf, evicted.at[1]), (vf, evicted.at[2]),
        ))
    ]

    scale = HEAD**-0.5

    def softmax(queries, keys):
        scores = lax.dot_general(queries, keys, (((1,), (1,)), ((), ())), preferred_element_type=jnp.float32) * scale
        seen = lax.broadcasted_iota(jnp.int32, (seq, seq), 0) >= lax.broadcasted_iota(jnp.int32, (seq, seq), 1)
        scores = jnp.where(seen, scores, jnp.float32(-1e30))
        grown = jnp.exp(scores - jnp.max(scores, axis=-1, keepdims=True))
        return grown / jnp.sum(grown, axis=-1, keepdims=True)

    def forward_attention():
        for h in range(heads):
            cols = pl.ds(h * HEAD, HEAD)
            low = softmax(qf[:, cols], kf[:, cols]).astype(jnp.bfloat16)
            ctx[:, cols] = jnp.dot(low, vf[:, cols], preferred_element_type=jnp.float32).astype(jnp.bfloat16)
        for off in range(8):
            for side in range(2):
                ctxp[pl.ds(slot(off, side) * rows, rows), :] = ctx[pl.ds(row_of(off, side), rows), :]

    def project(first, last):
        @pl.loop(first // TILE, last // TILE)
        def _(i):
            cols = pl.ds(pl.multiple_of(i * TILE, TILE), TILE)
            made = jnp.dot(ctxp[...], w[:, cols], preferred_element_type=jnp.float32).astype(jnp.bfloat16)
            part[:, :, cols] = made.reshape(part.shape[0], rows, TILE)

    def gather_grad(first, last):
        @pl.loop(first // TILE, last // TILE)
        def _(i):
            cols = pl.ds(pl.multiple_of(i * TILE, TILE), TILE)
            total[...] += lax.dot_general(
                g[:, :, cols].reshape(seq, TILE), w[:, cols], (((1,), (1,)), ((), ())), preferred_element_type=jnp.float32
            )

    def spread_grad():
        for off in range(8):
            for side in range(2):
                rows_here = pl.ds(slot(off, side) * rows, rows)
                gctx[pl.ds(row_of(off, side), rows), :] = total[rows_here, :].astype(jnp.bfloat16)

    def stash_probs():
        for h in range(heads):
            cols = pl.ds(h * HEAD, HEAD)
            attn = softmax(qs[:, cols], ks[:, cols])
            probs[h] = attn
            recon[:, cols] = jnp.dot(
                attn.astype(jnp.bfloat16), vs[:, cols], preferred_element_type=jnp.float32
            ).astype(jnp.bfloat16)

    def backward_attention():
        for h in range(heads):
            cols = pl.ds(h * HEAD, HEAD)
            grad, attn = gctx[:, cols], probs[h]
            dots = jnp.sum(
                grad.astype(jnp.float32) * recon[:, cols].astype(jnp.float32), axis=-1, keepdims=True
            )
            grad_probs = lax.dot_general(
                grad, vs[:, cols], (((1,), (1,)), ((), ())), preferred_element_type=jnp.float32
            )
            grad_scores = (attn * (grad_probs - dots)).astype(jnp.bfloat16)
            gout[0, :, cols] = (
                jnp.dot(grad_scores, ks[:, cols], preferred_element_type=jnp.float32) * scale
            ).astype(jnp.bfloat16)
            gout[1, :, cols] = (
                lax.dot_general(
                    grad_scores, qs[:, cols], (((0,), (0,)), ((), ())), preferred_element_type=jnp.float32
                )
                * scale
            ).astype(jnp.bfloat16)
            gout[2, :, cols] = lax.dot_general(
                attn.astype(jnp.bfloat16), grad, (((0,), (0,)), ((), ())), preferred_element_type=jnp.float32
            ).astype(jnp.bfloat16)

    def add(dst, terms, first, last):
        @pl.loop(0, (last - first) // STEP)
        def _(i):
            at = first + i * STEP
            total = part[dst, :, pl.ds(pl.multiple_of(at, STEP), STEP)].astype(jnp.float32)
            for ref, shift in terms:
                total += ref[:, pl.ds(pl.multiple_of(at - shift, STEP), STEP)].astype(jnp.float32)
            part[dst, :, pl.ds(pl.multiple_of(at, STEP), STEP)] = total.astype(jnp.bfloat16)

    def reduce_a(hop, way):
        off = (4 - hop) * (1 if way == 0 else -1) % 8
        here, middle = slot(off, 0), CUT // 2
        left, right = (0, middle), (middle, CUT)
        rsy[off].wait_recv()
        rsz[way, hop - 1, 0].wait_recv()
        if hop == 1:
            add(here, [(ya.at[off], 0), (za.at[way, 0], 0)], *(left, right)[way])
            add(here, [(ya.at[off], 0)], *(right, left)[way])
        else:
            add(here, [(ya.at[off], 0), (za.at[way, hop - 1], 0)], 0, CUT)
        rsz[way, hop, 0].start()

    def reduce_b(hop, stream, way):
        side = sides[stream]
        off = (4 - hop) * (1 if way == 0 else -1) % 8
        if hop > 0:
            rsz[way, hop - 1, stream].wait_recv()
            middle = CUT + wide_b // 2
            first, last = ((CUT, middle), (middle, width))[way] if hop == 1 else (CUT, width)
            add(slot(off, side), [(zb.at[way, hop - 1, side], CUT)], first, last)
        rsz[way, hop, stream].start()

    def gather_on(hop, stream, way):
        agz[way, hop, stream].wait_recv()
        if hop < 3:
            agz[way, hop + 1, stream].start()
        if stream == 0:
            agy[(-1 if way == 0 else 1) * (hop + 1) % 8 if hop < 3 else (4, way)].start()

    def act(what, *at):
        if what == "send":
            agz[at[0], 0, at[1]].start()
        elif what == "cross":
            agy["b"].start()
        elif what == "cross0":
            agy[0].start()
        elif what == "mirror":
            if at[0] < 3:
                loads[f"p{at[0]}"].wait()
            mir[at[0]].start()
        elif what == "forward":
            for name in ("q", "k", "v"):
                loads[name].wait()
            forward_attention()
        elif what == "crossed":
            agy["b"].wait_recv()
            for way in range(2):
                agz[way, 0, 2].start()
        elif what in ("project_b", "project_a"):
            if what == next(step[0] for step in PLAN if step[0].startswith("project")):
                for i in range(4):
                    loads[f"w{i}"].wait()
            project(*((0, CUT) if what == "project_a" else (CUT, width)))
        elif what == "part":
            rsy[at[0]].start()
        elif what == "gather":
            gather_on(*at)
        elif what == "reduce_b":
            reduce_b(*at)
        elif what == "reduce_a0":
            rsy[4].wait_recv()
            add(slot(4, 0), [(ya.at[4], 0)], 0, CUT)
            for way in range(2):
                rsz[way, 0, 0].start()
        elif what == "reduce_a":
            reduce_a(*at)
        elif what == "sum_b":
            for way in range(2):
                rsz[way, 3, 2].wait_recv()
            add(slot(0, 1), [(zb.at[0, 3, 1], CUT), (zb.at[1, 3, 1], CUT)], CUT, width)
            rsy["b"].start()
        elif what == "stash":
            for i in range(3):
                mir[i].wait_recv()
            stash_probs()
        elif what == "grad_b":
            gather_grad(CUT, width)
        elif what == "grad_a":
            for off in (0, 7, 1, 6, 2, 5, 3):
                agy[off].wait_recv()
            for way in range(2):
                agy[4, way].wait_recv()
            gather_grad(0, CUT)
        elif what == "backward":
            spread_grad()
            backward_attention()
            for i, ref in enumerate((gq_ref, gk_ref, gv_ref)):
                stores.append(pltpu.make_async_copy(gout.at[i], ref.at[0], store_sem.at[i]))
                stores[-1].start()

    barrier = pltpu.get_barrier_semaphore()
    for device in (up, down, across, mirror):
        pl.semaphore_signal(barrier, inc=1, device_id=device, device_id_type=MESH)
    pl.semaphore_wait(barrier, 4)

    loads["cot"].wait()
    total[...] = jnp.zeros_like(total)
    stores = []
    for step in PLAN:
        act(*step)

    loads["resid"].wait()
    rsy[0].wait_recv()
    for way in range(2):
        rsz[way, 3, 0].wait_recv()
        rsz[way, 3, 1].wait_recv()
    rsy["b"].wait_recv()

    def finish(first, last, refs, shift):
        @pl.loop(0, (last - first) // STEP)
        def _(i):
            cols = pl.ds(pl.multiple_of(first + i * STEP, STEP), STEP)
            total = part[slot(0, 0), :, cols].astype(jnp.float32)
            for ref in refs:
                total += ref[:, pl.ds(pl.multiple_of(first - shift + i * STEP, STEP), STEP)].astype(jnp.float32)
            out[:, cols] = (resid[:, cols].astype(jnp.float32) + total).astype(jnp.bfloat16)

    finish(0, CUT, (ya.at[0], za.at[0, 3], za.at[1, 3]), 0)
    finish(CUT, width, (yb, zb.at[0, 3, 0], zb.at[1, 3, 0]), CUT)
    last = pltpu.make_async_copy(out, out_ref.at[0], store_sem.at[3])
    last.start()

    for i, ref in enumerate((eq_ref, ek_ref, ev_ref)):
        mir[3 + i].wait_recv()
        stores.append(pltpu.make_async_copy(evicted.at[i], ref.at[0], store_sem.at[4 + i]))
        stores[-1].start()
    for copies in (agz, rsz, agy, rsy):
        for copy in copies.values():
            copy.wait_send()
    for copy in mir:
        copy.wait_send()
    for copy in stores:
        copy.wait()
    last.wait()


def place(*refs):
    count = len(refs) // 3
    sem_in, sem_out = refs[-2:]
    comes = [pltpu.make_async_copy(refs[i], refs[2 * count + i], sem_in.at[i]) for i in range(count)]
    goes = [pltpu.make_async_copy(refs[2 * count + i], refs[count + i], sem_out.at[i]) for i in range(count)]
    for copy in comes:
        copy.start()
    for i in range(count):
        comes[i].wait()
        goes[i].start()
    for copy in goes:
        copy.wait()


def per_device(q_fwd, k_fwd, v_fwd, q_park, k_park, v_park, resid, out_weight, cotangent):
    seq, features = q_fwd.shape[1:]
    rows, width = resid.shape[1:]
    slots = seq // rows
    heads = features // HEAD
    low = jnp.bfloat16
    block = jax.ShapeDtypeStruct(q_fwd.shape, low)
    anywhere = pl.BlockSpec(memory_space=pl.ANY)
    sems = pltpu.SemaphoreType.DMA
    made = pl.pallas_call(
        kernel,
        name="relay",
        out_shape=(jax.ShapeDtypeStruct(resid.shape, low),) + (block,) * 6,
        in_specs=[anywhere] * 9,
        out_specs=(anywhere,) * 7,
        scratch_shapes=[
            pltpu.VMEM((features, width), low),
            pltpu.VMEM((slots, rows, width), low),
            pltpu.VMEM((slots, rows, width), low),
            pltpu.VMEM((2, 4, rows, CUT), low),
            pltpu.VMEM((2, 4, 2, rows, width - CUT), low),
            pltpu.VMEM((8, rows, CUT), low),
            pltpu.VMEM((rows, width - CUT), low),
            *[pltpu.VMEM((seq, features), low) for _ in range(6)],
            pltpu.VMEM((3, seq, features), low),
            pltpu.VMEM((3, seq, features), low),
            pltpu.VMEM((rows, width), low),
            pltpu.VMEM((seq, features), low),
            pltpu.VMEM((seq, features), low),
            pltpu.VMEM((heads, seq, seq), jnp.float32),
            pltpu.VMEM((seq, features), low),
            pltpu.VMEM((seq, features), jnp.float32),
            pltpu.VMEM((seq, features), low),
            pltpu.VMEM((3, seq, features), low),
            pltpu.VMEM((rows, width), low),
            sems((12,)), sems((7,)), sems((24,)), sems((24,)), sems((10,)), sems((10,)),
            sems((24,)), sems((24,)), sems((9,)), sems((9,)), sems((6,)), sems((6,)),
        ],
        compiler_params=pltpu.CompilerParams(
            collective_id=0, has_side_effects=True, vmem_limit_bytes=56 * 2**20
        ),
    )(q_fwd, k_fwd, v_fwd, q_park, k_park, v_park, resid, out_weight, cotangent)
    return pl.pallas_call(
        place,
        name="place",
        out_shape=tuple(jax.ShapeDtypeStruct(x.shape, x.dtype) for x in made),
        in_specs=[anywhere] * 7,
        out_specs=(anywhere,) * 7,
        scratch_shapes=[pltpu.VMEM(x.shape, x.dtype) for x in made] + [sems((7,)), sems((7,))],
    )(*made)


def solution(mesh):
    placed = (P("pipe", None, "tensor"),) * 6 + (P("pipe", "tensor", None),) * 3
    return jax.shard_map(
        per_device,
        mesh=mesh,
        in_specs=placed,
        out_specs=(P("pipe", "tensor", None),) + (P("pipe", None, "tensor"),) * 6,
        check_vma=False,
    )
```

```python
import jax
import jax.numpy as jnp
from jax import lax
from jax.experimental import pallas as pl
from jax.experimental.pallas import tpu as pltpu
from jax.sharding import PartitionSpec as P

HEAD = 128
MESH = pl.DeviceIdType.MESH
CUT = 5120
TILE = 1024
STEP = 512
PLAN = (
    ("mirror", 0), ("cross",), ("send", 0, 1), ("send", 1, 0), ("send", 0, 0), ("send", 1, 1), ("forward",),
    ("project_b",), ("reduce_b", 0, 1, 1), ("mirror", 1), ("reduce_b", 0, 2, 0), ("project_a",), ("part", 3),
    ("reduce_b", 0, 1, 0), ("gather", 0, 0, 1), ("reduce_b", 0, 2, 1), ("gather", 0, 1, 1), ("gather", 0, 0, 0),
    ("crossed",), ("part", 4), ("part", 5), ("reduce_b", 1, 1, 1), ("reduce_b", 1, 2, 0), ("gather", 1, 0, 0),
    ("part", 6), ("part", 7), ("gather", 0, 1, 0), ("mirror", 2), ("reduce_b", 1, 2, 1), ("reduce_b", 1, 1, 0),
    ("gather", 1, 0, 1), ("reduce_a0",), ("gather", 0, 2, 0), ("part", 2), ("gather", 0, 2, 1), ("reduce_b", 2, 1, 1),
    ("gather", 2, 0, 0), ("part", 0), ("reduce_b", 2, 2, 0), ("reduce_b", 2, 2, 1), ("reduce_a", 1, 0),
    ("reduce_a", 1, 1), ("gather", 2, 0, 1), ("gather", 1, 1, 0), ("gather", 1, 2, 1), ("gather", 1, 2, 0),
    ("mirror", 3), ("reduce_a", 2, 0), ("gather", 1, 1, 1), ("reduce_b", 2, 1, 0), ("reduce_b", 3, 2, 0), ("part", 1),
    ("reduce_b", 3, 2, 1), ("cross0",), ("mirror", 4), ("reduce_a", 2, 1), ("gather", 3, 0, 1), ("gather", 2, 2, 1),
    ("gather", 2, 2, 0), ("gather", 2, 1, 0), ("gather", 3, 0, 0), ("gather", 2, 1, 1), ("stash",), ("mirror", 5),
    ("reduce_b", 3, 1, 0), ("reduce_a", 3, 0), ("reduce_b", 3, 1, 1), ("sum_b",), ("reduce_a", 3, 1), ("grad_a",),
    ("gather", 3, 1, 0), ("gather", 3, 2, 0), ("gather", 3, 1, 1), ("gather", 3, 2, 1), ("grad_b",), ("backward",),
)


def slot(off, side):
    return side * 8 + off % 8


def kernel(
    q_in, k_in, v_in, qp_in, kp_in, vp_in, resid_in, w_in, cot_in,
    out_ref, gq_ref, gk_ref, gv_ref, eq_ref, ek_ref, ev_ref,
    w, g, part, za, zb, ya, yb, qf, kf, vf, qs, ks, vs, parked, resid, ctx, ctxp, probs, recon, total, gctx,
    load_sem, agz_s, agz_r, agy_s, agy_r, rsz_s, rsz_r, rsy_s, rsy_r, mir_s, mir_r,
):
    width = w.shape[1]
    rows = resid.shape[0]
    seq = qf.shape[0]
    heads = qf.shape[1] // HEAD
    wide_b = width - CUT
    p, t = lax.axis_index("pipe"), lax.axis_index("tensor")
    z, line = lax.div(t, 2), lax.rem(t, 2)
    up = (p, lax.rem(z + 1, 8) * 2 + line)
    down = (p, lax.rem(z + 7, 8) * 2 + line)
    across = (p, z * 2 + 1 - line)
    mirror = (lax.axis_size("pipe") - 1 - p, t)
    ways = (up, down)

    def row_of(off, side):
        block = lax.rem(z + off % 8, 8) * 2 + lax.rem(line + side, 2)
        return pl.multiple_of(block * rows, rows)

    loads = {}

    def load(name, src, dst):
        loads[name] = pltpu.make_async_copy(src, dst, load_sem.at[len(loads)])
        loads[name].start()

    load("cot", cot_in.at[0], g.at[slot(0, 0)])
    for i, ref in enumerate((qp_in, kp_in, vp_in)):
        load(f"p{i}", ref.at[0], parked.at[i])
    load("q", q_in.at[0], qf)
    load("k", k_in.at[0], kf)
    load("v", v_in.at[0], vf)
    quarter = w.shape[0] // 4
    for i in range(4):
        load(f"w{i}", w_in.at[0, pl.ds(i * quarter, quarter)], w.at[pl.ds(i * quarter, quarter)])
    load("resid", resid_in.at[0], resid)

    def remote(src, dst, send, recv, device):
        return pltpu.make_async_remote_copy(
            src_ref=src, dst_ref=dst, send_sem=send, recv_sem=recv, device_id=device, device_id_type=MESH
        )

    cols_a = pl.ds(0, CUT)
    cols_b = pl.ds(CUT, wide_b)
    half_a = (pl.ds(0, CUT // 2), pl.ds(CUT // 2, CUT // 2))
    half_b = (pl.ds(CUT, wide_b // 2), pl.ds(CUT + wide_b // 2, wide_b // 2))
    half_zb = (pl.ds(0, wide_b // 2), pl.ds(wide_b // 2, wide_b // 2))
    sides = (0, 0, 1)

    agz, rsz = {}, {}
    for way in range(2):
        sign = -1 if way == 0 else 1
        for hop in range(4):
            for stream in range(3):
                n = (way * 4 + hop) * 3 + stream
                side = sides[stream]
                if hop < 3:
                    cols = cols_a if stream == 0 else cols_b
                else:
                    cols = half_a[way] if stream == 0 else half_b[way]
                agz[way, hop, stream] = remote(
                    g.at[slot(sign * hop, side), :, cols],
                    g.at[slot(sign * (hop + 1), side), :, cols],
                    agz_s.at[n], agz_r.at[n], ways[way],
                )
                if hop > 0:
                    cols = cols_a if stream == 0 else cols_b
                    land = za.at[way, hop] if stream == 0 else zb.at[way, hop, side]
                else:
                    cols = half_a[way] if stream == 0 else half_b[way]
                    land = za.at[way, hop, :, half_a[way]] if stream == 0 else zb.at[way, hop, side, :, half_zb[way]]
                rsz[way, hop, stream] = remote(
                    part.at[slot(-sign * (4 - hop), side), :, cols], land, rsz_s.at[n], rsz_r.at[n], ways[way]
                )
    agy, rsy = {}, {}
    for i, off in enumerate((0, 7, 1, 6, 2, 5, 3)):
        agy[off] = remote(
            g.at[slot(off, 0), :, cols_a], g.at[slot(off, 1), :, cols_a], agy_s.at[i], agy_r.at[i], across
        )
    for way in range(2):
        agy[4, way] = remote(
            g.at[slot(4, 0), :, half_a[way]], g.at[slot(4, 1), :, half_a[way]],
            agy_s.at[7 + way], agy_r.at[7 + way], across,
        )
    agy["b"] = remote(g.at[slot(0, 0), :, cols_b], g.at[slot(0, 1), :, cols_b], agy_s.at[9], agy_r.at[9], across)
    for off in range(8):
        rsy[off] = remote(part.at[slot(off, 1), :, cols_a], ya.at[off], rsy_s.at[off], rsy_r.at[off], across)
    rsy["b"] = remote(part.at[slot(0, 1), :, cols_b], yb, rsy_s.at[8], rsy_r.at[8], across)
    mir = [
        remote(src, dst, mir_s.at[i], mir_r.at[i], mirror)
        for i, (src, dst) in enumerate((
            (parked.at[0], qs), (parked.at[1], ks), (parked.at[2], vs),
            (qf, eq_ref.at[0]), (kf, ek_ref.at[0]), (vf, ev_ref.at[0]),
        ))
    ]

    scale = HEAD**-0.5

    def softmax(queries, keys):
        scores = lax.dot_general(queries, keys, (((1,), (1,)), ((), ())), preferred_element_type=jnp.float32) * scale
        seen = lax.broadcasted_iota(jnp.int32, (seq, seq), 0) >= lax.broadcasted_iota(jnp.int32, (seq, seq), 1)
        scores = jnp.where(seen, scores, jnp.float32(-1e30))
        grown = jnp.exp(scores - jnp.max(scores, axis=-1, keepdims=True))
        return grown / jnp.sum(grown, axis=-1, keepdims=True)

    def forward_attention():
        for h in range(heads):
            cols = pl.ds(h * HEAD, HEAD)
            low = softmax(qf[:, cols], kf[:, cols]).astype(jnp.bfloat16)
            ctx[:, cols] = jnp.dot(low, vf[:, cols], preferred_element_type=jnp.float32).astype(jnp.bfloat16)
        for off in range(8):
            for side in range(2):
                ctxp[pl.ds(slot(off, side) * rows, rows), :] = ctx[pl.ds(row_of(off, side), rows), :]

    def project(first, last):
        @pl.loop(first // TILE, last // TILE)
        def _(i):
            cols = pl.ds(pl.multiple_of(i * TILE, TILE), TILE)
            made = jnp.dot(ctxp[...], w[:, cols], preferred_element_type=jnp.float32).astype(jnp.bfloat16)
            part[:, :, cols] = made.reshape(part.shape[0], rows, TILE)

    def gather_grad(first, last):
        @pl.loop(first // TILE, last // TILE)
        def _(i):
            cols = pl.ds(pl.multiple_of(i * TILE, TILE), TILE)
            total[...] += lax.dot_general(
                g[:, :, cols].reshape(seq, TILE), w[:, cols], (((1,), (1,)), ((), ())), preferred_element_type=jnp.float32
            )

    def spread_grad():
        for off in range(8):
            for side in range(2):
                rows_here = pl.ds(slot(off, side) * rows, rows)
                gctx[pl.ds(row_of(off, side), rows), :] = total[rows_here, :].astype(jnp.bfloat16)

    def stash_probs():
        for h in range(heads):
            cols = pl.ds(h * HEAD, HEAD)
            attn = softmax(qs[:, cols], ks[:, cols])
            probs[h] = attn
            recon[:, cols] = jnp.dot(
                attn.astype(jnp.bfloat16), vs[:, cols], preferred_element_type=jnp.float32
            ).astype(jnp.bfloat16)

    def backward_attention():
        for h in range(heads):
            cols = pl.ds(h * HEAD, HEAD)
            grad, attn = gctx[:, cols], probs[h]
            dots = jnp.sum(
                grad.astype(jnp.float32) * recon[:, cols].astype(jnp.float32), axis=-1, keepdims=True
            )
            grad_probs = lax.dot_general(
                grad, vs[:, cols], (((1,), (1,)), ((), ())), preferred_element_type=jnp.float32
            )
            grad_scores = (attn * (grad_probs - dots)).astype(jnp.bfloat16)
            gq_ref[0, :, cols] = (
                jnp.dot(grad_scores, ks[:, cols], preferred_element_type=jnp.float32) * scale
            ).astype(jnp.bfloat16)
            gk_ref[0, :, cols] = (
                lax.dot_general(
                    grad_scores, qs[:, cols], (((0,), (0,)), ((), ())), preferred_element_type=jnp.float32
                )
                * scale
            ).astype(jnp.bfloat16)
            gv_ref[0, :, cols] = lax.dot_general(
                attn.astype(jnp.bfloat16), grad, (((0,), (0,)), ((), ())), preferred_element_type=jnp.float32
            ).astype(jnp.bfloat16)

    def add(dst, terms, first, last):
        @pl.loop(0, (last - first) // STEP)
        def _(i):
            at = first + i * STEP
            total = part[dst, :, pl.ds(pl.multiple_of(at, STEP), STEP)].astype(jnp.float32)
            for ref, shift in terms:
                total += ref[:, pl.ds(pl.multiple_of(at - shift, STEP), STEP)].astype(jnp.float32)
            part[dst, :, pl.ds(pl.multiple_of(at, STEP), STEP)] = total.astype(jnp.bfloat16)

    def reduce_a(hop, way):
        off = (4 - hop) * (1 if way == 0 else -1) % 8
        here, middle = slot(off, 0), CUT // 2
        left, right = (0, middle), (middle, CUT)
        rsy[off].wait_recv()
        rsz[way, hop - 1, 0].wait_recv()
        if hop == 1:
            add(here, [(ya.at[off], 0), (za.at[way, 0], 0)], *(left, right)[way])
            add(here, [(ya.at[off], 0)], *(right, left)[way])
        else:
            add(here, [(ya.at[off], 0), (za.at[way, hop - 1], 0)], 0, CUT)
        rsz[way, hop, 0].start()

    def reduce_b(hop, stream, way):
        side = sides[stream]
        off = (4 - hop) * (1 if way == 0 else -1) % 8
        if hop > 0:
            rsz[way, hop - 1, stream].wait_recv()
            middle = CUT + wide_b // 2
            first, last = ((CUT, middle), (middle, width))[way] if hop == 1 else (CUT, width)
            add(slot(off, side), [(zb.at[way, hop - 1, side], CUT)], first, last)
        rsz[way, hop, stream].start()

    def gather_on(hop, stream, way):
        agz[way, hop, stream].wait_recv()
        if hop < 3:
            agz[way, hop + 1, stream].start()
        if stream == 0:
            agy[(-1 if way == 0 else 1) * (hop + 1) % 8 if hop < 3 else (4, way)].start()

    def act(what, *at):
        if what == "send":
            agz[at[0], 0, at[1]].start()
        elif what == "cross":
            agy["b"].start()
        elif what == "cross0":
            agy[0].start()
        elif what == "mirror":
            if at[0] < 3:
                loads[f"p{at[0]}"].wait()
            mir[at[0]].start()
        elif what == "forward":
            for name in ("q", "k", "v"):
                loads[name].wait()
            forward_attention()
        elif what == "crossed":
            agy["b"].wait_recv()
            for way in range(2):
                agz[way, 0, 2].start()
        elif what in ("project_b", "project_a"):
            if what == next(step[0] for step in PLAN if step[0].startswith("project")):
                for i in range(4):
                    loads[f"w{i}"].wait()
            project(*((0, CUT) if what == "project_a" else (CUT, width)))
        elif what == "part":
            rsy[at[0]].start()
        elif what == "gather":
            gather_on(*at)
        elif what == "reduce_b":
            reduce_b(*at)
        elif what == "reduce_a0":
            rsy[4].wait_recv()
            add(slot(4, 0), [(ya.at[4], 0)], 0, CUT)
            for way in range(2):
                rsz[way, 0, 0].start()
        elif what == "reduce_a":
            reduce_a(*at)
        elif what == "sum_b":
            for way in range(2):
                rsz[way, 3, 2].wait_recv()
            add(slot(0, 1), [(zb.at[0, 3, 1], CUT), (zb.at[1, 3, 1], CUT)], CUT, width)
            rsy["b"].start()
        elif what == "stash":
            for i in range(3):
                mir[i].wait_recv()
            stash_probs()
        elif what == "grad_b":
            gather_grad(CUT, width)
        elif what == "grad_a":
            for off in (0, 7, 1, 6, 2, 5, 3):
                agy[off].wait_recv()
            for way in range(2):
                agy[4, way].wait_recv()
            gather_grad(0, CUT)
        elif what == "backward":
            spread_grad()
            backward_attention()

    barrier = pltpu.get_barrier_semaphore()
    for device in (up, down, across, mirror):
        pl.semaphore_signal(barrier, inc=1, device_id=device, device_id_type=MESH)
    pl.semaphore_wait(barrier, 4)

    loads["cot"].wait()
    total[...] = jnp.zeros_like(total)
    for step in PLAN:
        act(*step)

    loads["resid"].wait()
    rsy[0].wait_recv()
    for way in range(2):
        rsz[way, 3, 0].wait_recv()
        rsz[way, 3, 1].wait_recv()
    rsy["b"].wait_recv()

    def finish(first, last, refs, shift):
        @pl.loop(0, (last - first) // STEP)
        def _(i):
            cols = pl.ds(pl.multiple_of(first + i * STEP, STEP), STEP)
            total = part[slot(0, 0), :, cols].astype(jnp.float32)
            for ref in refs:
                total += ref[:, pl.ds(pl.multiple_of(first - shift + i * STEP, STEP), STEP)].astype(jnp.float32)
            out_ref[0, :, cols] = (resid[:, cols].astype(jnp.float32) + total).astype(jnp.bfloat16)

    finish(0, CUT, (ya.at[0], za.at[0, 3], za.at[1, 3]), 0)
    finish(CUT, width, (yb, zb.at[0, 3, 0], zb.at[1, 3, 0]), CUT)

    for i in range(3, 6):
        mir[i].wait_recv()
    for copies in (agz, rsz, agy, rsy):
        for copy in copies.values():
            copy.wait_send()
    for copy in mir:
        copy.wait_send()


def place(*refs):
    count = len(refs) // 2
    copies = [pltpu.make_async_copy(refs[i], refs[count + i], refs[-1].at[i]) for i in range(count)]
    for copy in copies:
        copy.start()
    for copy in copies:
        copy.wait()


def per_device(q_fwd, k_fwd, v_fwd, q_park, k_park, v_park, resid, out_weight, cotangent):
    seq, features = q_fwd.shape[1:]
    rows, width = resid.shape[1:]
    slots = seq // rows
    heads = features // HEAD
    low = jnp.bfloat16
    anywhere = pl.BlockSpec(memory_space=pl.ANY)
    sems = pltpu.SemaphoreType.DMA
    made = pl.pallas_call(
        kernel,
        name="relay",
        out_shape=(pltpu.VMEM(resid.shape, low),) + (pltpu.VMEM(q_fwd.shape, low),) * 6,
        in_specs=[pl.BlockSpec(memory_space=pltpu.HBM)] * 9,
        out_specs=(pl.BlockSpec(memory_space=pltpu.VMEM),) * 7,
        scratch_shapes=[
            pltpu.VMEM((features, width), low),
            pltpu.VMEM((slots, rows, width), low),
            pltpu.VMEM((slots, rows, width), low),
            pltpu.VMEM((2, 4, rows, CUT), low),
            pltpu.VMEM((2, 4, 2, rows, width - CUT), low),
            pltpu.VMEM((8, rows, CUT), low),
            pltpu.VMEM((rows, width - CUT), low),
            *[pltpu.VMEM((seq, features), low) for _ in range(6)],
            pltpu.VMEM((3, seq, features), low),
            pltpu.VMEM((rows, width), low),
            pltpu.VMEM((seq, features), low),
            pltpu.VMEM((seq, features), low),
            pltpu.VMEM((heads, seq, seq), jnp.float32),
            pltpu.VMEM((seq, features), low),
            pltpu.VMEM((seq, features), jnp.float32),
            pltpu.VMEM((seq, features), low),
            sems((12,)), sems((24,)), sems((24,)), sems((10,)), sems((10,)),
            sems((24,)), sems((24,)), sems((9,)), sems((9,)), sems((6,)), sems((6,)),
        ],
        compiler_params=pltpu.CompilerParams(
            collective_id=0, has_side_effects=True, vmem_limit_bytes=56 * 2**20
        ),
    )(q_fwd, k_fwd, v_fwd, q_park, k_park, v_park, resid, out_weight, cotangent)
    return pl.pallas_call(
        place,
        name="place",
        out_shape=tuple(jax.ShapeDtypeStruct(x.shape, x.dtype) for x in made),
        in_specs=[pl.BlockSpec(memory_space=pltpu.VMEM)] * 7,
        out_specs=(anywhere,) * 7,
        scratch_shapes=[sems((7,))],
    )(*(pltpu.with_memory_space_constraint(x, pltpu.VMEM) for x in made))


def solution(mesh):
    placed = (P("pipe", None, "tensor"),) * 6 + (P("pipe", "tensor", None),) * 3
    return jax.shard_map(
        per_device,
        mesh=mesh,
        in_specs=placed,
        out_specs=(P("pipe", "tensor", None),) + (P("pipe", None, "tensor"),) * 6,
        check_vma=False,
    )
```

```python
import jax
import jax.numpy as jnp
from jax import lax
from jax.experimental import pallas as pl
from jax.experimental.pallas import tpu as pltpu
from jax.sharding import PartitionSpec as P

HEAD = 128
MESH = pl.DeviceIdType.MESH
CUT = 5120
TILE = 1024
STEP = 512
PLAN = (
    ("mirror", 0), ("cross",), ("send", 0, 1), ("send", 1, 0), ("send", 0, 0), ("send", 1, 1), ("forward",),
    ("project_b",), ("reduce_b", 0, 1, 1), ("mirror", 1), ("reduce_b", 0, 2, 0), ("project_a",), ("part", 3),
    ("reduce_b", 0, 1, 0), ("gather", 0, 0, 1), ("reduce_b", 0, 2, 1), ("gather", 0, 1, 1), ("gather", 0, 0, 0),
    ("crossed",), ("part", 4), ("part", 5), ("reduce_b", 1, 1, 1), ("reduce_b", 1, 2, 0), ("gather", 1, 0, 0),
    ("part", 6), ("part", 7), ("gather", 0, 1, 0), ("mirror", 2), ("reduce_b", 1, 2, 1), ("reduce_b", 1, 1, 0),
    ("gather", 1, 0, 1), ("reduce_a0",), ("gather", 0, 2, 0), ("part", 2), ("gather", 0, 2, 1), ("reduce_b", 2, 1, 1),
    ("gather", 2, 0, 0), ("part", 0), ("reduce_b", 2, 2, 0), ("reduce_b", 2, 2, 1), ("reduce_a", 1, 0),
    ("reduce_a", 1, 1), ("gather", 2, 0, 1), ("gather", 1, 1, 0), ("gather", 1, 2, 1), ("gather", 1, 2, 0),
    ("mirror", 3), ("reduce_a", 2, 0), ("gather", 1, 1, 1), ("reduce_b", 2, 1, 0), ("reduce_b", 3, 2, 0), ("part", 1),
    ("reduce_b", 3, 2, 1), ("cross0",), ("mirror", 4), ("reduce_a", 2, 1), ("gather", 3, 0, 1), ("gather", 2, 2, 1),
    ("gather", 2, 2, 0), ("gather", 2, 1, 0), ("gather", 3, 0, 0), ("gather", 2, 1, 1), ("stash",), ("mirror", 5),
    ("reduce_b", 3, 1, 0), ("reduce_a", 3, 0), ("reduce_b", 3, 1, 1), ("sum_b",), ("reduce_a", 3, 1), ("grad_a",),
    ("gather", 3, 1, 0), ("gather", 3, 2, 0), ("gather", 3, 1, 1), ("gather", 3, 2, 1), ("grad_b",), ("backward",),
)


def slot(off, side):
    return side * 8 + off % 8


def kernel(
    q_in, k_in, v_in, qp_in, kp_in, vp_in, resid_in, w_in, cot_in,
    out_ref, gq_ref, gk_ref, gv_ref, eq_ref, ek_ref, ev_ref,
    w, g, part, za, zb, ya, yb, qf, kf, vf, qs, ks, vs, parked, resid, ctx, ctxp, probs, recon, total, gctx,
    load_sem, agz_s, agz_r, agy_s, agy_r, rsz_s, rsz_r, rsy_s, rsy_r, mir_s, mir_r,
):
    width = w.shape[1]
    rows = resid.shape[0]
    seq = qf.shape[0]
    heads = qf.shape[1] // HEAD
    wide_b = width - CUT
    p, t = lax.axis_index("pipe"), lax.axis_index("tensor")
    z, line = lax.div(t, 2), lax.rem(t, 2)
    up = (p, lax.rem(z + 1, 8) * 2 + line)
    down = (p, lax.rem(z + 7, 8) * 2 + line)
    across = (p, z * 2 + 1 - line)
    mirror = (lax.axis_size("pipe") - 1 - p, t)
    ways = (up, down)

    def row_of(off, side):
        block = lax.rem(z + off % 8, 8) * 2 + lax.rem(line + side, 2)
        return pl.multiple_of(block * rows, rows)

    barrier = pltpu.get_barrier_semaphore()
    for device in (up, down, across, mirror):
        pl.semaphore_signal(barrier, inc=1, device_id=device, device_id_type=MESH)

    loads = {}

    def load(name, src, dst):
        loads[name] = pltpu.make_async_copy(src, dst, load_sem.at[len(loads)])
        loads[name].start()

    load("cot", cot_in.at[0], g.at[slot(0, 0)])
    load("q", q_in.at[0], qf)
    load("k", k_in.at[0], kf)
    load("v", v_in.at[0], vf)
    deep = w.shape[0] // 2
    for name, cols in (("b", pl.ds(CUT, wide_b)), ("a", pl.ds(0, CUT))):
        for i in range(2):
            depth = pl.ds(i * deep, deep)
            load(f"w{name}{i}", w_in.at[0, depth, cols], w.at[depth, cols])
    for i, ref in enumerate((qp_in, kp_in, vp_in)):
        load(f"p{i}", ref.at[0], parked.at[i])
    load("resid", resid_in.at[0], resid)

    def remote(src, dst, send, recv, device):
        return pltpu.make_async_remote_copy(
            src_ref=src, dst_ref=dst, send_sem=send, recv_sem=recv, device_id=device, device_id_type=MESH
        )

    cols_a = pl.ds(0, CUT)
    cols_b = pl.ds(CUT, wide_b)
    half_a = (pl.ds(0, CUT // 2), pl.ds(CUT // 2, CUT // 2))
    half_b = (pl.ds(CUT, wide_b // 2), pl.ds(CUT + wide_b // 2, wide_b // 2))
    half_zb = (pl.ds(0, wide_b // 2), pl.ds(wide_b // 2, wide_b // 2))
    sides = (0, 0, 1)

    agz, rsz = {}, {}
    for way in range(2):
        sign = -1 if way == 0 else 1
        for hop in range(4):
            for stream in range(3):
                n = (way * 4 + hop) * 3 + stream
                side = sides[stream]
                if hop < 3:
                    cols = cols_a if stream == 0 else cols_b
                else:
                    cols = half_a[way] if stream == 0 else half_b[way]
                agz[way, hop, stream] = remote(
                    g.at[slot(sign * hop, side), :, cols],
                    g.at[slot(sign * (hop + 1), side), :, cols],
                    agz_s.at[n], agz_r.at[n], ways[way],
                )
                if hop > 0:
                    cols = cols_a if stream == 0 else cols_b
                    land = za.at[way, hop] if stream == 0 else zb.at[way, hop, side]
                else:
                    cols = half_a[way] if stream == 0 else half_b[way]
                    land = za.at[way, hop, :, half_a[way]] if stream == 0 else zb.at[way, hop, side, :, half_zb[way]]
                rsz[way, hop, stream] = remote(
                    part.at[slot(-sign * (4 - hop), side), :, cols], land, rsz_s.at[n], rsz_r.at[n], ways[way]
                )
    agy, rsy = {}, {}
    for i, off in enumerate((0, 7, 1, 6, 2, 5, 3)):
        agy[off] = remote(
            g.at[slot(off, 0), :, cols_a], g.at[slot(off, 1), :, cols_a], agy_s.at[i], agy_r.at[i], across
        )
    for way in range(2):
        agy[4, way] = remote(
            g.at[slot(4, 0), :, half_a[way]], g.at[slot(4, 1), :, half_a[way]],
            agy_s.at[7 + way], agy_r.at[7 + way], across,
        )
    agy["b"] = remote(g.at[slot(0, 0), :, cols_b], g.at[slot(0, 1), :, cols_b], agy_s.at[9], agy_r.at[9], across)
    for off in range(8):
        rsy[off] = remote(part.at[slot(off, 1), :, cols_a], ya.at[off], rsy_s.at[off], rsy_r.at[off], across)
    rsy["b"] = remote(part.at[slot(0, 1), :, cols_b], yb, rsy_s.at[8], rsy_r.at[8], across)
    mir = [
        remote(src, dst, mir_s.at[i], mir_r.at[i], mirror)
        for i, (src, dst) in enumerate((
            (parked.at[0], qs), (parked.at[1], ks), (parked.at[2], vs),
            (qf, eq_ref.at[0]), (kf, ek_ref.at[0]), (vf, ev_ref.at[0]),
        ))
    ]

    scale = HEAD**-0.5

    def softmax(queries, keys):
        scores = lax.dot_general(queries, keys, (((1,), (1,)), ((), ())), preferred_element_type=jnp.float32) * scale
        seen = lax.broadcasted_iota(jnp.int32, (seq, seq), 0) >= lax.broadcasted_iota(jnp.int32, (seq, seq), 1)
        scores = jnp.where(seen, scores, jnp.float32(-1e30))
        grown = jnp.exp(scores - jnp.max(scores, axis=-1, keepdims=True))
        return grown / jnp.sum(grown, axis=-1, keepdims=True)

    def forward_attention():
        for h in range(heads):
            cols = pl.ds(h * HEAD, HEAD)
            low = softmax(qf[:, cols], kf[:, cols]).astype(jnp.bfloat16)
            ctx[:, cols] = jnp.dot(low, vf[:, cols], preferred_element_type=jnp.float32).astype(jnp.bfloat16)
        for off in range(8):
            for side in range(2):
                ctxp[pl.ds(slot(off, side) * rows, rows), :] = ctx[pl.ds(row_of(off, side), rows), :]

    def project(first, last):
        @pl.loop(first // TILE, last // TILE)
        def _(i):
            cols = pl.ds(pl.multiple_of(i * TILE, TILE), TILE)
            made = jnp.dot(ctxp[...], w[:, cols], preferred_element_type=jnp.float32).astype(jnp.bfloat16)
            part[:, :, cols] = made.reshape(part.shape[0], rows, TILE)

    def gather_grad(first, last):
        @pl.loop(first // TILE, last // TILE)
        def _(i):
            cols = pl.ds(pl.multiple_of(i * TILE, TILE), TILE)
            total[...] += lax.dot_general(
                g[:, :, cols].reshape(seq, TILE), w[:, cols], (((1,), (1,)), ((), ())), preferred_element_type=jnp.float32
            )

    def spread_grad():
        for off in range(8):
            for side in range(2):
                rows_here = pl.ds(slot(off, side) * rows, rows)
                gctx[pl.ds(row_of(off, side), rows), :] = total[rows_here, :].astype(jnp.bfloat16)

    def stash_probs():
        for h in range(heads):
            cols = pl.ds(h * HEAD, HEAD)
            attn = softmax(qs[:, cols], ks[:, cols])
            probs[h] = attn
            recon[:, cols] = jnp.dot(
                attn.astype(jnp.bfloat16), vs[:, cols], preferred_element_type=jnp.float32
            ).astype(jnp.bfloat16)

    def backward_attention():
        for h in range(heads):
            cols = pl.ds(h * HEAD, HEAD)
            grad, attn = gctx[:, cols], probs[h]
            dots = jnp.sum(
                grad.astype(jnp.float32) * recon[:, cols].astype(jnp.float32), axis=-1, keepdims=True
            )
            grad_probs = lax.dot_general(
                grad, vs[:, cols], (((1,), (1,)), ((), ())), preferred_element_type=jnp.float32
            )
            grad_scores = (attn * (grad_probs - dots)).astype(jnp.bfloat16)
            gq_ref[0, :, cols] = (
                jnp.dot(grad_scores, ks[:, cols], preferred_element_type=jnp.float32) * scale
            ).astype(jnp.bfloat16)
            gk_ref[0, :, cols] = (
                lax.dot_general(
                    grad_scores, qs[:, cols], (((0,), (0,)), ((), ())), preferred_element_type=jnp.float32
                )
                * scale
            ).astype(jnp.bfloat16)
            gv_ref[0, :, cols] = lax.dot_general(
                attn.astype(jnp.bfloat16), grad, (((0,), (0,)), ((), ())), preferred_element_type=jnp.float32
            ).astype(jnp.bfloat16)

    def add(dst, terms, first, last):
        @pl.loop(0, (last - first) // STEP)
        def _(i):
            at = first + i * STEP
            total = part[dst, :, pl.ds(pl.multiple_of(at, STEP), STEP)].astype(jnp.float32)
            for ref, shift in terms:
                total += ref[:, pl.ds(pl.multiple_of(at - shift, STEP), STEP)].astype(jnp.float32)
            part[dst, :, pl.ds(pl.multiple_of(at, STEP), STEP)] = total.astype(jnp.bfloat16)

    def reduce_a(hop, way):
        off = (4 - hop) * (1 if way == 0 else -1) % 8
        here, middle = slot(off, 0), CUT // 2
        left, right = (0, middle), (middle, CUT)
        rsy[off].wait_recv()
        rsz[way, hop - 1, 0].wait_recv()
        if hop == 1:
            add(here, [(ya.at[off], 0), (za.at[way, 0], 0)], *(left, right)[way])
            add(here, [(ya.at[off], 0)], *(right, left)[way])
        else:
            add(here, [(ya.at[off], 0), (za.at[way, hop - 1], 0)], 0, CUT)
        rsz[way, hop, 0].start()

    def reduce_b(hop, stream, way):
        side = sides[stream]
        off = (4 - hop) * (1 if way == 0 else -1) % 8
        if hop > 0:
            rsz[way, hop - 1, stream].wait_recv()
            middle = CUT + wide_b // 2
            first, last = ((CUT, middle), (middle, width))[way] if hop == 1 else (CUT, width)
            add(slot(off, side), [(zb.at[way, hop - 1, side], CUT)], first, last)
        rsz[way, hop, stream].start()

    def gather_on(hop, stream, way):
        agz[way, hop, stream].wait_recv()
        if hop < 3:
            agz[way, hop + 1, stream].start()
        if stream == 0:
            agy[(-1 if way == 0 else 1) * (hop + 1) % 8 if hop < 3 else (4, way)].start()

    def act(what, *at):
        if what == "send":
            agz[at[0], 0, at[1]].start()
        elif what == "cross":
            agy["b"].start()
        elif what == "cross0":
            agy[0].start()
        elif what == "mirror":
            if at[0] < 3:
                loads[f"p{at[0]}"].wait()
            mir[at[0]].start()
        elif what == "forward":
            for name in ("q", "k", "v"):
                loads[name].wait()
            forward_attention()
            total[...] = jnp.zeros_like(total)
        elif what == "crossed":
            agy["b"].wait_recv()
            for way in range(2):
                agz[way, 0, 2].start()
        elif what in ("project_b", "project_a"):
            for i in range(2):
                loads[f"w{what[-1]}{i}"].wait()
            project(*((0, CUT) if what == "project_a" else (CUT, width)))
        elif what == "part":
            rsy[at[0]].start()
        elif what == "gather":
            gather_on(*at)
        elif what == "reduce_b":
            reduce_b(*at)
        elif what == "reduce_a0":
            rsy[4].wait_recv()
            add(slot(4, 0), [(ya.at[4], 0)], 0, CUT)
            for way in range(2):
                rsz[way, 0, 0].start()
        elif what == "reduce_a":
            reduce_a(*at)
        elif what == "sum_b":
            for way in range(2):
                rsz[way, 3, 2].wait_recv()
            add(slot(0, 1), [(zb.at[0, 3, 1], CUT), (zb.at[1, 3, 1], CUT)], CUT, width)
            rsy["b"].start()
        elif what == "stash":
            for i in range(3):
                mir[i].wait_recv()
            stash_probs()
        elif what == "grad_b":
            gather_grad(CUT, width)
        elif what == "grad_a":
            for off in (0, 7, 1, 6, 2, 5, 3):
                agy[off].wait_recv()
            for way in range(2):
                agy[4, way].wait_recv()
            gather_grad(0, CUT)
        elif what == "backward":
            spread_grad()
            backward_attention()

    pl.semaphore_wait(barrier, 4)
    loads["cot"].wait()
    for step in PLAN:
        act(*step)

    def finish(first, last, refs, shift):
        @pl.loop(0, (last - first) // STEP)
        def _(i):
            cols = pl.ds(pl.multiple_of(first + i * STEP, STEP), STEP)
            total = part[slot(0, 0), :, cols].astype(jnp.float32)
            for ref in refs:
                total += ref[:, pl.ds(pl.multiple_of(first - shift + i * STEP, STEP), STEP)].astype(jnp.float32)
            out_ref[0, :, cols] = (resid[:, cols].astype(jnp.float32) + total).astype(jnp.bfloat16)

    loads["resid"].wait()
    for copies in (agz, rsz, agy, rsy):
        for copy in copies.values():
            copy.wait_send()
    for copy in mir:
        copy.wait_send()
    for i in range(3, 6):
        mir[i].wait_recv()
    rsy["b"].wait_recv()
    for way in range(2):
        rsz[way, 3, 1].wait_recv()
    finish(CUT, width, (yb, zb.at[0, 3, 0], zb.at[1, 3, 0]), CUT)
    rsy[0].wait_recv()
    for way in range(2):
        rsz[way, 3, 0].wait_recv()
    finish(0, CUT, (ya.at[0], za.at[0, 3], za.at[1, 3]), 0)


def place(*refs):
    count = len(refs) // 2
    copies = [pltpu.make_async_copy(refs[i], refs[count + i], refs[-1].at[i]) for i in range(count)]
    for copy in copies:
        copy.start()
    for copy in copies:
        copy.wait()


def per_device(q_fwd, k_fwd, v_fwd, q_park, k_park, v_park, resid, out_weight, cotangent):
    seq, features = q_fwd.shape[1:]
    rows, width = resid.shape[1:]
    slots = seq // rows
    heads = features // HEAD
    low = jnp.bfloat16
    anywhere = pl.BlockSpec(memory_space=pl.ANY)
    sems = pltpu.SemaphoreType.DMA
    made = pl.pallas_call(
        kernel,
        name="relay",
        out_shape=(pltpu.VMEM(resid.shape, low),) + (pltpu.VMEM(q_fwd.shape, low),) * 6,
        in_specs=[pl.BlockSpec(memory_space=pltpu.HBM)] * 9,
        out_specs=(pl.BlockSpec(memory_space=pltpu.VMEM),) * 7,
        scratch_shapes=[
            pltpu.VMEM((features, width), low),
            pltpu.VMEM((slots, rows, width), low),
            pltpu.VMEM((slots, rows, width), low),
            pltpu.VMEM((2, 4, rows, CUT), low),
            pltpu.VMEM((2, 4, 2, rows, width - CUT), low),
            pltpu.VMEM((8, rows, CUT), low),
            pltpu.VMEM((rows, width - CUT), low),
            *[pltpu.VMEM((seq, features), low) for _ in range(6)],
            pltpu.VMEM((3, seq, features), low),
            pltpu.VMEM((rows, width), low),
            pltpu.VMEM((seq, features), low),
            pltpu.VMEM((seq, features), low),
            pltpu.VMEM((heads, seq, seq), jnp.float32),
            pltpu.VMEM((seq, features), low),
            pltpu.VMEM((seq, features), jnp.float32),
            pltpu.VMEM((seq, features), low),
            sems((12,)), sems((24,)), sems((24,)), sems((10,)), sems((10,)),
            sems((24,)), sems((24,)), sems((9,)), sems((9,)), sems((6,)), sems((6,)),
        ],
        compiler_params=pltpu.CompilerParams(
            collective_id=0, has_side_effects=True, vmem_limit_bytes=56 * 2**20
        ),
    )(q_fwd, k_fwd, v_fwd, q_park, k_park, v_park, resid, out_weight, cotangent)
    return pl.pallas_call(
        place,
        name="place",
        out_shape=tuple(jax.ShapeDtypeStruct(x.shape, x.dtype) for x in made),
        in_specs=[pl.BlockSpec(memory_space=pltpu.VMEM)] * 7,
        out_specs=(anywhere,) * 7,
        scratch_shapes=[sems((7,))],
    )(*(pltpu.with_memory_space_constraint(x, pltpu.VMEM) for x in made))


def solution(mesh):
    placed = (P("pipe", None, "tensor"),) * 6 + (P("pipe", "tensor", None),) * 3
    return jax.shard_map(
        per_device,
        mesh=mesh,
        in_specs=placed,
        out_specs=(P("pipe", "tensor", None),) + (P("pipe", None, "tensor"),) * 6,
        check_vma=False,
    )
```

```python
import jax
import jax.numpy as jnp
from jax import lax
from jax.experimental import pallas as pl
from jax.experimental.pallas import tpu as pltpu
from jax.sharding import PartitionSpec as P

HEAD = 128
MESH = pl.DeviceIdType.MESH
CUT = 5120
TILE = 1024
STEP = 512
PLAN = (
    ("mirror", 0), ("cross",), ("send", 0, 1), ("send", 1, 0), ("send", 0, 0), ("send", 1, 1), ("forward",),
    ("project_b",), ("reduce_b", 0, 1, 1), ("mirror", 1), ("reduce_b", 0, 2, 0), ("project_a",), ("part", 3),
    ("reduce_b", 0, 1, 0), ("gather", 0, 0, 1), ("reduce_b", 0, 2, 1), ("gather", 0, 1, 1), ("gather", 0, 0, 0),
    ("crossed",), ("part", 4), ("part", 5), ("reduce_b", 1, 1, 1), ("reduce_b", 1, 2, 0), ("gather", 1, 0, 0),
    ("part", 6), ("part", 7), ("gather", 0, 1, 0), ("mirror", 2), ("reduce_b", 1, 2, 1), ("reduce_b", 1, 1, 0),
    ("gather", 1, 0, 1), ("reduce_a0",), ("gather", 0, 2, 0), ("part", 2), ("gather", 0, 2, 1), ("reduce_b", 2, 1, 1),
    ("gather", 2, 0, 0), ("part", 0), ("reduce_b", 2, 2, 0), ("reduce_b", 2, 2, 1), ("reduce_a", 1, 0),
    ("reduce_a", 1, 1), ("gather", 2, 0, 1), ("gather", 1, 1, 0), ("gather", 1, 2, 1), ("gather", 1, 2, 0),
    ("mirror", 3), ("reduce_a", 2, 0), ("gather", 1, 1, 1), ("reduce_b", 2, 1, 0), ("reduce_b", 3, 2, 0), ("part", 1),
    ("reduce_b", 3, 2, 1), ("cross0",), ("mirror", 4), ("reduce_a", 2, 1), ("gather", 3, 0, 1), ("gather", 2, 2, 1),
    ("gather", 2, 2, 0), ("gather", 2, 1, 0), ("gather", 3, 0, 0), ("gather", 2, 1, 1), ("stash",), ("mirror", 5),
    ("reduce_b", 3, 1, 0), ("reduce_a", 3, 0), ("reduce_b", 3, 1, 1), ("sum_b",), ("reduce_a", 3, 1), ("grad_a",),
    ("gather", 3, 1, 0), ("gather", 3, 2, 0), ("gather", 3, 1, 1), ("gather", 3, 2, 1), ("grad_b",), ("backward",),
)


def slot(off, side):
    return side * 8 + off % 8


def kernel(
    q_in, k_in, v_in, qp_in, kp_in, vp_in, resid_in, w_in, cot_in,
    out_ref, gq_ref, gk_ref, gv_ref, eq_ref, ek_ref, ev_ref,
    w, g, part, za, zb, ya, yb, qf, kf, vf, qs, ks, vs, parked, resid, ctx, ctxp, probs, recon, total, gctx,
    load_sem, agz_s, agz_r, agy_s, agy_r, rsz_s, rsz_r, rsy_s, rsy_r, mir_s, mir_r,
):
    width = w.shape[1]
    rows = resid.shape[0]
    seq = qf.shape[0]
    heads = qf.shape[1] // HEAD
    wide_b = width - CUT
    p, t = lax.axis_index("pipe"), lax.axis_index("tensor")
    z, line = lax.div(t, 2), lax.rem(t, 2)
    up = (p, lax.rem(z + 1, 8) * 2 + line)
    down = (p, lax.rem(z + 7, 8) * 2 + line)
    across = (p, z * 2 + 1 - line)
    mirror = (lax.axis_size("pipe") - 1 - p, t)
    ways = (up, down)

    def row_of(off, side):
        block = lax.rem(z + off % 8, 8) * 2 + lax.rem(line + side, 2)
        return pl.multiple_of(block * rows, rows)

    barrier = pltpu.get_barrier_semaphore()
    for device in (up, down, across, mirror):
        pl.semaphore_signal(barrier, inc=1, device_id=device, device_id_type=MESH)

    loads = {}

    def load(name, src, dst):
        loads[name] = pltpu.make_async_copy(src, dst, load_sem.at[len(loads)])
        loads[name].start()

    load("cot", cot_in.at[0], g.at[slot(0, 0)])
    load("q", q_in.at[0], qf)
    load("k", k_in.at[0], kf)
    load("v", v_in.at[0], vf)
    deep = w.shape[0] // 2
    for name, cols in (("b", pl.ds(CUT, wide_b)), ("a", pl.ds(0, CUT))):
        for i in range(2):
            depth = pl.ds(i * deep, deep)
            load(f"w{name}{i}", w_in.at[0, depth, cols], w.at[depth, cols])
    for i, ref in enumerate((qp_in, kp_in, vp_in)):
        load(f"p{i}", ref.at[0], parked.at[i])
    load("resid", resid_in.at[0], resid)

    def remote(src, dst, send, recv, device):
        return pltpu.make_async_remote_copy(
            src_ref=src, dst_ref=dst, send_sem=send, recv_sem=recv, device_id=device, device_id_type=MESH
        )

    cols_a = pl.ds(0, CUT)
    cols_b = pl.ds(CUT, wide_b)
    half_a = (pl.ds(0, CUT // 2), pl.ds(CUT // 2, CUT // 2))
    half_b = (pl.ds(CUT, wide_b // 2), pl.ds(CUT + wide_b // 2, wide_b // 2))
    half_zb = (pl.ds(0, wide_b // 2), pl.ds(wide_b // 2, wide_b // 2))
    sides = (0, 0, 1)

    agz, rsz = {}, {}
    for way in range(2):
        sign = -1 if way == 0 else 1
        for hop in range(4):
            for stream in range(3):
                n = (way * 4 + hop) * 3 + stream
                side = sides[stream]
                if hop < 3:
                    cols = cols_a if stream == 0 else cols_b
                else:
                    cols = half_a[way] if stream == 0 else half_b[way]
                agz[way, hop, stream] = remote(
                    g.at[slot(sign * hop, side), :, cols],
                    g.at[slot(sign * (hop + 1), side), :, cols],
                    agz_s.at[n], agz_r.at[n], ways[way],
                )
                if hop > 0:
                    cols = cols_a if stream == 0 else cols_b
                    land = za.at[way, hop] if stream == 0 else zb.at[way, hop, side]
                else:
                    cols = half_a[way] if stream == 0 else half_b[way]
                    land = za.at[way, hop, :, half_a[way]] if stream == 0 else zb.at[way, hop, side, :, half_zb[way]]
                rsz[way, hop, stream] = remote(
                    part.at[slot(-sign * (4 - hop), side), :, cols], land, rsz_s.at[n], rsz_r.at[n], ways[way]
                )
    agy, rsy = {}, {}
    for i, off in enumerate((0, 7, 1, 6, 2, 5, 3)):
        agy[off] = remote(
            g.at[slot(off, 0), :, cols_a], g.at[slot(off, 1), :, cols_a], agy_s.at[i], agy_r.at[i], across
        )
    for way in range(2):
        agy[4, way] = remote(
            g.at[slot(4, 0), :, half_a[way]], g.at[slot(4, 1), :, half_a[way]],
            agy_s.at[7 + way], agy_r.at[7 + way], across,
        )
    agy["b"] = remote(g.at[slot(0, 0), :, cols_b], g.at[slot(0, 1), :, cols_b], agy_s.at[9], agy_r.at[9], across)
    for off in range(8):
        rsy[off] = remote(part.at[slot(off, 1), :, cols_a], ya.at[off], rsy_s.at[off], rsy_r.at[off], across)
    rsy["b"] = remote(part.at[slot(0, 1), :, cols_b], yb, rsy_s.at[8], rsy_r.at[8], across)
    mir = [
        remote(src, dst, mir_s.at[i], mir_r.at[i], mirror)
        for i, (src, dst) in enumerate((
            (parked.at[0], qs), (parked.at[1], ks), (parked.at[2], vs),
            (qf, eq_ref.at[0]), (kf, ek_ref.at[0]), (vf, ev_ref.at[0]),
        ))
    ]

    scale = HEAD**-0.5

    def softmax(queries, keys):
        scores = lax.dot_general(queries, keys, (((1,), (1,)), ((), ())), preferred_element_type=jnp.float32) * scale
        seen = lax.broadcasted_iota(jnp.int32, (seq, seq), 0) >= lax.broadcasted_iota(jnp.int32, (seq, seq), 1)
        scores = jnp.where(seen, scores, jnp.float32(-1e30))
        grown = jnp.exp(scores - jnp.max(scores, axis=-1, keepdims=True))
        return grown / jnp.sum(grown, axis=-1, keepdims=True)

    def forward_attention():
        for h in range(heads):
            cols = pl.ds(h * HEAD, HEAD)
            low = softmax(qf[:, cols], kf[:, cols]).astype(jnp.bfloat16)
            ctx[:, cols] = jnp.dot(low, vf[:, cols], preferred_element_type=jnp.float32).astype(jnp.bfloat16)
        for off in range(8):
            for side in range(2):
                ctxp[pl.ds(slot(off, side) * rows, rows), :] = ctx[pl.ds(row_of(off, side), rows), :]

    def project(first, last):
        tile = 1792 if (last - first) % 1792 == 0 else 2560

        @pl.loop(0, (last - first) // tile)
        def _(i):
            cols = pl.ds(pl.multiple_of(first + i * tile, HEAD), tile)
            made = jnp.dot(ctxp[...], w[:, cols], preferred_element_type=jnp.float32).astype(jnp.bfloat16)
            part[:, :, cols] = made.reshape(part.shape[0], rows, tile)

    def gather_grad(first, last):
        @pl.loop(first // TILE, last // TILE)
        def _(i):
            cols = pl.ds(pl.multiple_of(i * TILE, TILE), TILE)
            total[...] += lax.dot_general(
                g[:, :, cols].reshape(seq, TILE), w[:, cols], (((1,), (1,)), ((), ())), preferred_element_type=jnp.float32
            )

    def spread_grad():
        for off in range(8):
            for side in range(2):
                rows_here = pl.ds(slot(off, side) * rows, rows)
                gctx[pl.ds(row_of(off, side), rows), :] = total[rows_here, :].astype(jnp.bfloat16)

    def stash_probs():
        for h in range(heads):
            cols = pl.ds(h * HEAD, HEAD)
            attn = softmax(qs[:, cols], ks[:, cols])
            probs[h] = attn
            recon[:, cols] = jnp.dot(
                attn.astype(jnp.bfloat16), vs[:, cols], preferred_element_type=jnp.float32
            ).astype(jnp.bfloat16)

    def backward_attention():
        for h in range(heads):
            cols = pl.ds(h * HEAD, HEAD)
            grad, attn = gctx[:, cols], probs[h]
            dots = jnp.sum(
                grad.astype(jnp.float32) * recon[:, cols].astype(jnp.float32), axis=-1, keepdims=True
            )
            grad_probs = lax.dot_general(
                grad, vs[:, cols], (((1,), (1,)), ((), ())), preferred_element_type=jnp.float32
            )
            grad_scores = (attn * (grad_probs - dots)).astype(jnp.bfloat16)
            gq_ref[0, :, cols] = (
                jnp.dot(grad_scores, ks[:, cols], preferred_element_type=jnp.float32) * scale
            ).astype(jnp.bfloat16)
            gk_ref[0, :, cols] = (
                lax.dot_general(
                    grad_scores, qs[:, cols], (((0,), (0,)), ((), ())), preferred_element_type=jnp.float32
                )
                * scale
            ).astype(jnp.bfloat16)
            gv_ref[0, :, cols] = lax.dot_general(
                attn.astype(jnp.bfloat16), grad, (((0,), (0,)), ((), ())), preferred_element_type=jnp.float32
            ).astype(jnp.bfloat16)

    def add(dst, terms, first, last):
        @pl.loop(0, (last - first) // STEP)
        def _(i):
            at = first + i * STEP
            total = part[dst, :, pl.ds(pl.multiple_of(at, STEP), STEP)].astype(jnp.float32)
            for ref, shift in terms:
                total += ref[:, pl.ds(pl.multiple_of(at - shift, STEP), STEP)].astype(jnp.float32)
            part[dst, :, pl.ds(pl.multiple_of(at, STEP), STEP)] = total.astype(jnp.bfloat16)

    def reduce_a(hop, way):
        off = (4 - hop) * (1 if way == 0 else -1) % 8
        here, middle = slot(off, 0), CUT // 2
        left, right = (0, middle), (middle, CUT)
        rsy[off].wait_recv()
        rsz[way, hop - 1, 0].wait_recv()
        if hop == 1:
            add(here, [(ya.at[off], 0), (za.at[way, 0], 0)], *(left, right)[way])
            add(here, [(ya.at[off], 0)], *(right, left)[way])
        else:
            add(here, [(ya.at[off], 0), (za.at[way, hop - 1], 0)], 0, CUT)
        rsz[way, hop, 0].start()

    def reduce_b(hop, stream, way):
        side = sides[stream]
        off = (4 - hop) * (1 if way == 0 else -1) % 8
        if hop > 0:
            rsz[way, hop - 1, stream].wait_recv()
            middle = CUT + wide_b // 2
            first, last = ((CUT, middle), (middle, width))[way] if hop == 1 else (CUT, width)
            add(slot(off, side), [(zb.at[way, hop - 1, side], CUT)], first, last)
        rsz[way, hop, stream].start()

    def gather_on(hop, stream, way):
        agz[way, hop, stream].wait_recv()
        if hop < 3:
            agz[way, hop + 1, stream].start()
        if stream == 0:
            agy[(-1 if way == 0 else 1) * (hop + 1) % 8 if hop < 3 else (4, way)].start()

    def act(what, *at):
        if what == "send":
            agz[at[0], 0, at[1]].start()
        elif what == "cross":
            agy["b"].start()
        elif what == "cross0":
            agy[0].start()
        elif what == "mirror":
            if at[0] < 3:
                loads[f"p{at[0]}"].wait()
            mir[at[0]].start()
        elif what == "forward":
            for name in ("q", "k", "v"):
                loads[name].wait()
            forward_attention()
            total[...] = jnp.zeros_like(total)
        elif what == "crossed":
            agy["b"].wait_recv()
            for way in range(2):
                agz[way, 0, 2].start()
        elif what in ("project_b", "project_a"):
            for i in range(2):
                loads[f"w{what[-1]}{i}"].wait()
            project(*((0, CUT) if what == "project_a" else (CUT, width)))
        elif what == "part":
            rsy[at[0]].start()
        elif what == "gather":
            gather_on(*at)
        elif what == "reduce_b":
            reduce_b(*at)
        elif what == "reduce_a0":
            rsy[4].wait_recv()
            add(slot(4, 0), [(ya.at[4], 0)], 0, CUT)
            for way in range(2):
                rsz[way, 0, 0].start()
        elif what == "reduce_a":
            reduce_a(*at)
        elif what == "sum_b":
            for way in range(2):
                rsz[way, 3, 2].wait_recv()
            add(slot(0, 1), [(zb.at[0, 3, 1], CUT), (zb.at[1, 3, 1], CUT)], CUT, width)
            rsy["b"].start()
        elif what == "stash":
            for i in range(3):
                mir[i].wait_recv()
            stash_probs()
        elif what == "grad_b":
            gather_grad(CUT, width)
        elif what == "grad_a":
            for off in (0, 7, 1, 6, 2, 5, 3):
                agy[off].wait_recv()
            for way in range(2):
                agy[4, way].wait_recv()
            gather_grad(0, CUT)
        elif what == "backward":
            spread_grad()
            backward_attention()

    pl.semaphore_wait(barrier, 4)
    loads["cot"].wait()
    for step in PLAN:
        act(*step)

    def finish(first, last, refs, shift):
        @pl.loop(0, (last - first) // STEP)
        def _(i):
            cols = pl.ds(pl.multiple_of(first + i * STEP, STEP), STEP)
            total = part[slot(0, 0), :, cols].astype(jnp.float32)
            for ref in refs:
                total += ref[:, pl.ds(pl.multiple_of(first - shift + i * STEP, STEP), STEP)].astype(jnp.float32)
            out_ref[0, :, cols] = (resid[:, cols].astype(jnp.float32) + total).astype(jnp.bfloat16)

    loads["resid"].wait()
    for copies in (agz, rsz, agy, rsy):
        for copy in copies.values():
            copy.wait_send()
    for copy in mir:
        copy.wait_send()
    for i in range(3, 6):
        mir[i].wait_recv()
    rsy["b"].wait_recv()
    for way in range(2):
        rsz[way, 3, 1].wait_recv()
    finish(CUT, width, (yb, zb.at[0, 3, 0], zb.at[1, 3, 0]), CUT)
    rsy[0].wait_recv()
    for way in range(2):
        rsz[way, 3, 0].wait_recv()
    finish(0, CUT, (ya.at[0], za.at[0, 3], za.at[1, 3]), 0)


def place(*refs):
    count = len(refs) // 2
    copies = [pltpu.make_async_copy(refs[i], refs[count + i], refs[-1].at[i]) for i in range(count)]
    for copy in copies:
        copy.start()
    for copy in copies:
        copy.wait()


def per_device(q_fwd, k_fwd, v_fwd, q_park, k_park, v_park, resid, out_weight, cotangent):
    seq, features = q_fwd.shape[1:]
    rows, width = resid.shape[1:]
    slots = seq // rows
    heads = features // HEAD
    low = jnp.bfloat16
    anywhere = pl.BlockSpec(memory_space=pl.ANY)
    sems = pltpu.SemaphoreType.DMA
    made = pl.pallas_call(
        kernel,
        name="relay",
        out_shape=(pltpu.VMEM(resid.shape, low),) + (pltpu.VMEM(q_fwd.shape, low),) * 6,
        in_specs=[pl.BlockSpec(memory_space=pltpu.HBM)] * 9,
        out_specs=(pl.BlockSpec(memory_space=pltpu.VMEM),) * 7,
        scratch_shapes=[
            pltpu.VMEM((features, width), low),
            pltpu.VMEM((slots, rows, width), low),
            pltpu.VMEM((slots, rows, width), low),
            pltpu.VMEM((2, 4, rows, CUT), low),
            pltpu.VMEM((2, 4, 2, rows, width - CUT), low),
            pltpu.VMEM((8, rows, CUT), low),
            pltpu.VMEM((rows, width - CUT), low),
            *[pltpu.VMEM((seq, features), low) for _ in range(6)],
            pltpu.VMEM((3, seq, features), low),
            pltpu.VMEM((rows, width), low),
            pltpu.VMEM((seq, features), low),
            pltpu.VMEM((seq, features), low),
            pltpu.VMEM((heads, seq, seq), jnp.float32),
            pltpu.VMEM((seq, features), low),
            pltpu.VMEM((seq, features), jnp.float32),
            pltpu.VMEM((seq, features), low),
            sems((12,)), sems((24,)), sems((24,)), sems((10,)), sems((10,)),
            sems((24,)), sems((24,)), sems((9,)), sems((9,)), sems((6,)), sems((6,)),
        ],
        compiler_params=pltpu.CompilerParams(
            collective_id=0, has_side_effects=True, vmem_limit_bytes=56 * 2**20
        ),
    )(q_fwd, k_fwd, v_fwd, q_park, k_park, v_park, resid, out_weight, cotangent)
    return pl.pallas_call(
        place,
        name="place",
        out_shape=tuple(jax.ShapeDtypeStruct(x.shape, x.dtype) for x in made),
        in_specs=[pl.BlockSpec(memory_space=pltpu.VMEM)] * 7,
        out_specs=(anywhere,) * 7,
        scratch_shapes=[sems((7,))],
    )(*(pltpu.with_memory_space_constraint(x, pltpu.VMEM) for x in made))


def solution(mesh):
    placed = (P("pipe", None, "tensor"),) * 6 + (P("pipe", "tensor", None),) * 3
    return jax.shard_map(
        per_device,
        mesh=mesh,
        in_specs=placed,
        out_specs=(P("pipe", "tensor", None),) + (P("pipe", None, "tensor"),) * 6,
        check_vma=False,
    )
```
